128 devices in a mesh: circ: 32 (over z, x, y_hi), rad: 2 (over y_lo), half: 2 (over core).
Axes of the slice: x: 4, y: 4 (y_hi: 2, y_lo: 2; y = y_hi * 2 + y_lo), z: 4, core: 2. Of those that a mesh axis runs over, the one named last changes fastest.
Arguments:
- state: float32 [5, 96, 512, 256], P(None, 'half', 'circ', 'rad'), may hold values from -6 to 6
- offsets: int32 [3], replicated, may hold values from 1 to 511, as said below
- pml_zone: int32 [96], P('half'), may hold values from 0 to 1, as said below
Outputs:
- advanced: float32 [5, 96, 512, 256], P(None, 'half', 'circ', 'rad')
- increment: float32 [5, 96, 512, 256], P(None, 'half', 'circ', 'rad')
The draws below stay inside these ranges and needn't reach their ends.
Inputs may be any that keep to these rules, and one draw needn't show every extreme that they name: `pml_zone`: 1 on an inlet zone of the first planes and an outlet zone of the last planes, each 4 to 13 planes thick, 0 elsewhere. No offset is a multiple of 16; in some order the three sections' offsets lie in [496, 512), in [0, 16) and in [256, 272).
All inputs are finite; a program needn't handle non-finite values.
Results may differ from the reference program's by a relative error of at most 0.00002.
Values sent between devices are 32-bit elements; how exact they have to be, the bound alone decides.
No kernel may reach another device: no remote copies, remote signals or barrier semaphores. Data moves between devices by JAX's collectives and lax.ppermute only.
A program may use at most 128 MiB of HBM per device.

```python
import jax
import jax.numpy as jnp
from jax import lax

AXH = 48
CC = 16
SECTIONS = 3
NA = 96
NC = 512
NR = 256


def draw_pml_zone(key, part):
    key = jax.random.fold_in(key, 7)
    inlet_key, outlet_key = jax.random.split(key)
    inlet = jax.random.randint(inlet_key, (), 1 + AXH // 16, 2 + AXH // 4)
    outlet = jax.random.randint(outlet_key, (), 1 + AXH // 16, 2 + AXH // 4)
    planes = jnp.arange(NA, dtype=jnp.int32)
    return ((planes < inlet) | (planes >= NA - outlet)).astype(jnp.int32)


def draw_offsets(key, part):
    key = jax.random.fold_in(key, 11)
    order_key, within_key = jax.random.split(key)
    cycle_blocks = NC // CC
    starts = jnp.array([(cycle_blocks - 1) * CC, 0, cycle_blocks // 2 * CC], dtype=jnp.int32)
    order = jax.random.permutation(order_key, 3)
    within = jax.random.randint(within_key, (3,), 1, CC, dtype=jnp.int32)
    return (starts[order] + within).astype(jnp.int32)


def steps_of(key, dims, cuts, low, top_value):
    def one(dim, shards_of):
        draws = jax.random.uniform(jax.random.fold_in(jax.random.fold_in(key, 6), dim), (shards_of,), jnp.float32, low / len(cuts), top_value / len(cuts))
        return jnp.repeat(jnp.exp(draws), dims[dim] // shards_of).reshape((-1,) + (1,) * (len(dims) - dim - 1))

    level = one(*cuts[0])
    for cut in cuts[1:]:
        level = level * one(*cut)
    return level


def noise(stream_key, shape, spread, reach, pieces=(), kind=jnp.bfloat16):
    values = jax.random.normal(stream_key, shape, jnp.float32) * spread
    if len(pieces) > 0:
        values = steps_of(stream_key, shape, pieces, -0.22, 0.18) * values
    return jnp.clip(values, min=-reach, max=reach).astype(kind)


def setup_inputs(seed: int = 0) -> dict:
    arg_keys = jax.random.split(jax.random.key(seed), 4)
    state = noise(arg_keys[0], (5, NA, NC, NR), 1.0, 6.0, ((1, 2), (2, 32), (3, 2)), jnp.float32)
    offsets = draw_offsets(jax.random.fold_in(arg_keys[3], 71), 0)
    pml_zone = draw_pml_zone(jax.random.fold_in(arg_keys[3], 71), 0)
    return {"state": state, "offsets": offsets, "pml_zone": pml_zone}


coeffs = (0.872756993962, -0.286511173973, 0.090320001280, -0.020779405824, 0.002484594688)
mach = 0.3
step_size = 0.25
damping = 0.8
section_a = (0.0, -5.0 / 9.0, -153.0 / 128.0)
section_b = (1.0 / 3.0, 15.0 / 16.0, 8.0 / 15.0)


def derive(padded, axis, count):
    summed = None
    for distance, weight in enumerate(coeffs, start=1):
        higher = lax.slice_in_dim(padded, 5 + distance, 5 + distance + count, axis=axis)
        lowered = lax.slice_in_dim(padded, 5 - distance, 5 - distance + count, axis=axis)
        part_term = weight * (higher - lowered)
        summed = part_term if summed is None else summed + part_term
    return summed


def tendency(state, offset, pml_zone):
    rotor = state[:, :AXH]
    stator = state[:, AXH:]
    ghost_upper = jnp.roll(stator[:, :5], -offset, axis=2)
    ghost_lower = jnp.roll(rotor[:, AXH - 5:], offset, axis=2)
    zeros_rim = jnp.zeros_like(ghost_upper)
    axial = jnp.concatenate([
        derive(jnp.concatenate([zeros_rim, rotor, ghost_upper], axis=1), 1, AXH),
        derive(jnp.concatenate([ghost_lower, stator, zeros_rim], axis=1), 1, AXH)], axis=1)
    circ_pair = state[2:5:2]
    beside_all = jnp.concatenate([circ_pair[:, :, NC - 5:], circ_pair, circ_pair[:, :, :5]], axis=2)
    circ = derive(beside_all, 2, NC)
    beside = jnp.pad(state[3:5], ((0, 0), (0, 0), (0, 0), (5, 5)))
    radial = derive(beside, 3, NR)
    divergence = axial[1] + circ[0] + radial[0]
    rates = jnp.stack([
        mach * axial[0] + divergence,
        mach * axial[1] + axial[4],
        mach * axial[2] + circ[1],
        mach * axial[3] + radial[1],
        mach * axial[4] + divergence])
    sigma = damping * pml_zone.astype(jnp.float32)
    return -rates - sigma[None, :, None, None] * state


def reference(state, offsets, pml_zone):
    change = jnp.zeros_like(state)
    for section in range(SECTIONS):
        change = section_a[section] * change + step_size * tendency(state, offsets[section], pml_zone)
        state = state + section_b[section] * change
    return state, change
```

```python
import functools

import jax
import jax.numpy as jnp
import numpy as np
from jax import lax
from jax.experimental import pallas as pl
from jax.experimental.pallas import tpu as pltpu
from jax.sharding import PartitionSpec as P

SECTIONS = 3
F, A, C, L = 5, 48, 16, 128
ROWS = F * A * C
FIELD = A * C
W = 5

coeffs = (0.872756993962, -0.286511173973, 0.09032000128, -0.020779405824, 0.002484594688)
mach = 0.3
step_size = 0.25
damping = 0.8
section_a = (0.0, -5.0 / 9.0, -153.0 / 128.0)
section_b = (1.0 / 3.0, 15.0 / 16.0, 8.0 / 15.0)
HI = lax.Precision.HIGHEST


def radial_matrices():
    band = np.zeros((L, L), np.float32)
    pick = np.zeros((2, 8, L), np.float32)
    place = np.zeros((2, 8, L), np.float32)
    for k, c in enumerate(coeffs, start=1):
        for i in range(L):
            if i + k < L:
                band[i + k, i] = c
            elif i + k - L < W:
                place[0, i + k - L, i] = c
            if i - k >= 0:
                band[i - k, i] = -c
            else:
                place[1, i - k + W, i] = -c
    for j in range(W):
        pick[0, j, L - W + j] = 1.0
        pick[1, j, j] = 1.0
    return band, pick, place


def rows_of(f, a):
    return pl.ds(pl.multiple_of(f * FIELD + a * C, C), C)


def pack(q_ref, pick_ref, east_ref, odd_ref, rad_ref, face_ref):
    even = lax.rem(lax.axis_index("circ"), 2) == 0
    for g, f in enumerate((2, 4)):
        for c in range(W):
            head = q_ref[pl.ds(f * FIELD + c, A, stride=C), :]
            tail = q_ref[pl.ds(f * FIELD + C - W + c, A, stride=C), :]
            row = (g * W + c) * A
            east_ref[row : row + A, :] = jnp.where(even, tail, head)
            odd_ref[row : row + A, :] = jnp.where(even, head, tail)
    rad_ref[...] = lax.dot_general(
        pick_ref[lax.axis_index("rad")],
        q_ref[3 * FIELD :, :],
        (((1,), (1,)), ((), ())),
        precision=HI,
        preferred_element_type=jnp.float32,
    )
    rotor = lax.axis_index("half") == 0
    for f in range(F):
        for m in range(W):
            a = jnp.where(rotor, A - 1 - m, m)
            row = (f * W + m) * C
            face_ref[row : row + C, :] = q_ref[rows_of(f, a), :]


MESSAGES = [
    jax.ShapeDtypeStruct((2 * W * A, L), jnp.float32),
    jax.ShapeDtypeStruct((2 * W * A, L), jnp.float32),
    jax.ShapeDtypeStruct((8, 2 * FIELD), jnp.float32),
    jax.ShapeDtypeStruct((F * W * C, L), jnp.float32),
]
FIELDS = jax.ShapeDtypeStruct((ROWS, L), jnp.float32)
VM = pl.BlockSpec(memory_space=pltpu.VMEM)
SM = pl.BlockSpec(memory_space=pltpu.SMEM)


def local_kernel(section, pml_ref, band_ref, q_ref, *refs):
    inc_ref = refs[0] if section else None
    out_ref, pad = refs[-2:]
    zero = jnp.zeros((W * C, L), jnp.float32)
    span = (A + 2 * W) * C
    for f in range(F):
        pad[f * span : f * span + W * C, :] = zero
        pad[f * span + W * C : f * span + W * C + FIELD, :] = q_ref[f * FIELD : (f + 1) * FIELD, :]
        pad[(f + 1) * span - W * C : (f + 1) * span, :] = zero
    cell = lax.broadcasted_iota(jnp.int32, (C, L), 0)
    up = [jnp.where(cell < C - k, c, 0.0) for k, c in enumerate(coeffs, start=1)]
    down = [jnp.where(cell >= k, c, 0.0) for k, c in enumerate(coeffs, start=1)]

    def circ(x):
        total = None
        for k in range(1, W + 1):
            term = up[k - 1] * pltpu.roll(x, C - k, 0) - down[k - 1] * pltpu.roll(x, k, 0)
            total = term if total is None else total + term
        return total

    B = 4

    def step(n, carry):
        a0 = n * B
        axial = []
        here = []
        for f in range(F):
            planes = [
                pad[pl.ds(pl.multiple_of(f * span + (a0 + d) * C, C), C), :] for d in range(B + 2 * W)
            ]
            here.append(planes[W : W + B])
            axial.append(
                [
                    sum(c * (planes[W + p + k] - planes[W + p - k]) for k, c in enumerate(coeffs, start=1))
                    for p in range(B)
                ]
            )
        radial = jnp.dot(
            jnp.concatenate(here[3] + here[4], axis=0),
            band_ref[...],
            precision=HI,
            preferred_element_type=jnp.float32,
        )
        for p in range(B):
            rad3 = radial[p * C : (p + 1) * C]
            rad4 = radial[(B + p) * C : (B + p + 1) * C]
            div = axial[1][p] + circ(here[2][p]) + rad3
            rates = [
                mach * axial[0][p] + div,
                mach * axial[1][p] + axial[4][p],
                mach * axial[2][p] + circ(here[4][p]),
                mach * axial[3][p] + rad4,
                mach * axial[4][p] + div,
            ]
            sigma = damping * pml_ref[a0 + p].astype(jnp.float32)
            for f in range(F):
                rows = rows_of(f, a0 + p)
                value = -step_size * (rates[f] + sigma * here[f][p])
                if section:
                    value = value + section_a[section] * inc_ref[rows, :]
                out_ref[rows, :] = value
        return carry

    lax.fori_loop(0, A // B, step, 0)


def finish_kernel(
    section, last, offsets_ref, pick_ref, place_ref, q_ref, part_ref, east_ref, odd_ref, rim_ref, own_ref, next_ref, *refs
):
    b = section_b[section]
    if last:
        new_ref, inc_ref, rim = refs
    else:
        new_ref, inc_ref, *messages, rim = refs
    even = lax.rem(lax.axis_index("circ"), 2) == 0
    rotor = lax.axis_index("half") == 0
    rim[...] = lax.dot_general(
        rim_ref[...],
        place_ref[lax.axis_index("rad")],
        (((0,), (0,)), ((), ())),
        precision=HI,
        preferred_element_type=jnp.float32,
    )
    sub = lax.broadcasted_iota(jnp.int32, (8, L), 0)
    low_w = [jnp.where(sub < W - d, -coeffs[W - 1 - d], 0.0) for d in range(W)]
    high_w = [jnp.where(sub >= 8 - k, c, 0.0) for k, c in enumerate(coeffs, start=1)]

    def circ(a, g):
        first, skip = (0, 0) if g == 0 else (2, 3)
        rows = pl.ds(first * A + a, 8, stride=A)
        east, odd = east_ref[rows, :], odd_ref[rows, :]
        low = jnp.where(even, odd, east)
        high = jnp.where(even, east, odd)
        lower = upper = None
        for d in range(W):
            turn = (8 - d - skip) % 8
            term = low_w[d] * (pltpu.roll(low, turn, 0) if turn else low)
            lower = term if lower is None else lower + term
        for k in range(1, W + 1):
            turn = (8 - k - skip) % 8
            term = high_w[k - 1] * (pltpu.roll(high, turn, 0) if turn else high)
            upper = term if upper is None else upper + term
        return jnp.concatenate([lower, upper], axis=0)

    def step(a, carry):
        div = circ(a, 0) + rim[rows_of(0, a), :]
        extra = [div, None, circ(a, 1), rim[rows_of(1, a), :], div]
        for f in range(F):
            rows = rows_of(f, a)
            value = part_ref[rows, :]
            if extra[f] is not None:
                value = value - step_size * extra[f]
            inc_ref[rows, :] = value
            new_ref[rows, :] = q_ref[rows, :] + b * value
        return carry

    lax.fori_loop(0, A, step, 0, unroll=2)

    shift = lax.rem(offsets_ref[section], C)
    start = jnp.where(rotor, shift, C - shift)
    turn = 2 * C - start
    sign = jnp.where(rotor, 1.0, -1.0)
    ghost = []
    for f in range(F):
        planes = []
        for m in range(W):
            row = (f * W + m) * C
            own, beyond = own_ref[row : row + C, :], next_ref[row : row + C, :]
            both = jnp.concatenate([jnp.where(rotor, own, beyond), jnp.where(rotor, beyond, own)], axis=0)
            planes.append(pltpu.roll(both, turn, 0)[:C])
        ghost.append(planes)
    for i in range(W):
        a = jnp.where(rotor, A - 1 - i, i)
        axial = [sign * sum(coeffs[k - 1] * ghost[f][k - 1 - i] for k in range(i + 1, W + 1)) for f in range(F)]
        extra = [
            mach * axial[0] + axial[1],
            mach * axial[1] + axial[4],
            mach * axial[2],
            mach * axial[3],
            mach * axial[4] + axial[1],
        ]
        for f in range(F):
            rows = rows_of(f, a)
            delta = -step_size * extra[f]
            inc_ref[rows, :] += delta
            new_ref[rows, :] += b * delta
    if not last:
        pack(new_ref, pick_ref, *messages)


def swap_faces(face, blocks):
    count = lax.axis_size("circ")
    pairs = []
    for i in range(count):
        j = (i + blocks) % count
        pairs += [(2 * i, 2 * j + 1), (2 * j + 1, 2 * i)]
    return lax.ppermute(face, ("circ", "half"), pairs)


def exchange(messages, blocks):
    east, odd, rad, face = messages
    count = lax.axis_size("circ")
    return (
        lax.ppermute(east, "circ", [(i, i ^ 1) for i in range(count)]),
        lax.ppermute(odd, "circ", [(i, (i + (1 if i % 2 else -1)) % count) for i in range(count)]),
        lax.ppermute(rad, "rad", [(0, 1), (1, 0)]),
        swap_faces(face, blocks),
        swap_faces(face, blocks + 1),
    )


def march(kinds, q, offsets, pml_zone, messages):
    band, pick, place = radial_matrices()
    inc = None
    for section in range(SECTIONS):
        last = section == SECTIONS - 1
        arrived = exchange(messages, (-1, 0, C)[kinds[section]])
        part = pl.pallas_call(
            functools.partial(local_kernel, section),
            out_shape=FIELDS,
            in_specs=[SM] + [VM] * (3 if section else 2),
            out_specs=VM,
            scratch_shapes=[pltpu.VMEM((F * (A + 2 * W) * C, L), jnp.float32)],
            cost_estimate=pl.CostEstimate(flops=20_000_000, bytes_accessed=3 * ROWS * L * 4, transcendentals=0),
            name=f"local{section}",
        )(pml_zone, band, q, *([inc] if section else []))
        q, inc, *messages = pl.pallas_call(
            functools.partial(finish_kernel, section, last),
            out_shape=[FIELDS, FIELDS] + ([] if last else MESSAGES),
            in_specs=[SM] + [VM] * 9,
            out_specs=[VM] * (2 if last else 6),
            scratch_shapes=[pltpu.VMEM((2 * FIELD, L), jnp.float32)],
            name=f"finish{section}",
        )(offsets, pick, place, q, part, *arrived)
    return q, inc


def pack_kernel(q_ref, pick_ref, *messages):
    pack(q_ref, pick_ref, *messages)


def body(state, offsets, pml_zone):
    q = state.reshape(ROWS, L)
    messages = pl.pallas_call(
        pack_kernel,
        out_shape=MESSAGES,
        in_specs=[VM] * 2,
        out_specs=[VM] * 4,
        name="pack",
    )(q, radial_matrices()[1])
    place = offsets // C
    kind = jnp.where(place == 0, 1, jnp.where(place == C, 2, 0))
    order = kind[0] * 2 + kind[1] - (kind[1] > kind[0]).astype(jnp.int32)
    orders = [(i, j, 3 - i - j) for i in range(3) for j in range(3) if i != j]
    q, inc = lax.switch(
        order,
        [functools.partial(march, kinds) for kinds in orders],
        q,
        offsets,
        pml_zone,
        messages,
    )
    return q.reshape(state.shape), inc.reshape(state.shape)


def solution(mesh):
    return jax.shard_map(
        body,
        mesh=mesh,
        in_specs=(P(None, "half", "circ", "rad"), P(), P("half")),
        out_specs=(P(None, "half", "circ", "rad"), P(None, "half", "circ", "rad")),
        check_vma=False,
    )
```

```python
import functools

import jax
import jax.numpy as jnp
import numpy as np
from jax import lax
from jax.experimental import pallas as pl
from jax.experimental.pallas import tpu as pltpu
from jax.sharding import PartitionSpec as P

SECTIONS = 3
F, A, C, L = 5, 48, 16, 128
ROWS = F * A * C
FIELD = A * C
W = 5
GROUP = 6 * C
PARAMS = pltpu.CompilerParams(vmem_limit_bytes=24 << 20)

coeffs = (0.872756993962, -0.286511173973, 0.09032000128, -0.020779405824, 0.002484594688)
mach = 0.3
step_size = 0.25
damping = 0.8
section_a = (0.0, -5.0 / 9.0, -153.0 / 128.0)
section_b = (1.0 / 3.0, 15.0 / 16.0, 8.0 / 15.0)
HI = lax.Precision.HIGHEST


def band_matrix():
    band = np.zeros((L, L), np.float32)
    for k, c in enumerate(coeffs, start=1):
        band += c * (np.eye(L, k=-k) - np.eye(L, k=k)).astype(np.float32)
    return band


def rows_of(f, a):
    return pl.ds(pl.multiple_of(f * FIELD + a * C, C), C)


def total_of(terms):
    total = terms[0]
    for term in terms[1:]:
        total = total + term
    return total


def pack(q_ref, east_ref, odd_ref, rad_ref, face_ref):
    even = lax.rem(lax.axis_index("circ"), 2) == 0
    low_rad = lax.axis_index("rad") == 0
    rotor = lax.axis_index("half") == 0
    for g, f in enumerate((2, 4)):
        head = [q_ref[pl.ds(f * FIELD + c, A, stride=C), :] for c in range(W)]
        tail = [q_ref[pl.ds(f * FIELD + C - W + c, A, stride=C), :] for c in range(W)]
        for i in range(W):
            onward = total_of([-coeffs[i + W - c - 1] * tail[c] for c in range(i, W)])
            back = total_of([coeffs[c + W - i - 1] * head[c] for c in range(i + 1)])
            row = (g * W + i) * A
            east_ref[row : row + A, :] = jnp.where(even, onward, back)
            odd_ref[row : row + A, :] = jnp.where(even, back, onward)

    lane = lax.broadcasted_iota(jnp.int32, (GROUP, L), 1)
    first = jnp.where(low_rad, W, 0)
    rims = jnp.zeros((GROUP, L), jnp.float32)
    for n in range(2 * FIELD // GROUP):
        x = q_ref[3 * FIELD + n * GROUP : 3 * FIELD + (n + 1) * GROUP, :]
        rims = jnp.where((lane >= 8 * n) & (lane < 8 * n + W), pltpu.roll(x, first + 8 * n, 1), rims)
    slot = lax.rem(lane, 8)
    onward, back = [], []
    for d in range(W):
        c = coeffs[W - 1 - d]
        onward.append(jnp.where(slot + d < W, -c, 0.0) * (pltpu.roll(rims, L - d, 1) if d else rims))
        back.append(jnp.where((slot >= d) & (slot < W), c, 0.0) * (pltpu.roll(rims, d, 1) if d else rims))
    rad_ref[...] = jnp.where(low_rad, total_of(onward), total_of(back))

    for f in range(F):
        for m in range(W):
            a = jnp.where(rotor, A - 1 - m, m)
            row = (f * W + m) * C
            face_ref[row : row + C, :] = q_ref[rows_of(f, a), :]


MESSAGES = [
    jax.ShapeDtypeStruct((2 * W * A, L), jnp.float32),
    jax.ShapeDtypeStruct((2 * W * A, L), jnp.float32),
    jax.ShapeDtypeStruct((GROUP, L), jnp.float32),
    jax.ShapeDtypeStruct((F * W * C, L), jnp.float32),
]
FIELDS = jax.ShapeDtypeStruct((ROWS, L), jnp.float32)
VM = pl.BlockSpec(memory_space=pltpu.VMEM)
SM = pl.BlockSpec(memory_space=pltpu.SMEM)


def local_kernel(section, pml_ref, band_ref, q_ref, *refs):
    inc_ref = refs[0] if section else None
    out_ref, pad = refs[-2:]
    zero = jnp.zeros((W * C, L), jnp.float32)
    span = (A + 2 * W) * C
    for f in range(F):
        pad[f * span : f * span + W * C, :] = zero
        pad[f * span + W * C : f * span + W * C + FIELD, :] = q_ref[f * FIELD : (f + 1) * FIELD, :]
        pad[(f + 1) * span - W * C : (f + 1) * span, :] = zero
    cell = lax.broadcasted_iota(jnp.int32, (C, L), 0)
    up = [jnp.where(cell < C - k, c, 0.0) for k, c in enumerate(coeffs, start=1)]
    down = [jnp.where(cell >= k, c, 0.0) for k, c in enumerate(coeffs, start=1)]

    def circ(x):
        total = None
        for k in range(1, W + 1):
            term = up[k - 1] * pltpu.roll(x, C - k, 0) - down[k - 1] * pltpu.roll(x, k, 0)
            total = term if total is None else total + term
        return total

    B = 4

    def step(n, carry):
        a0 = n * B
        axial = []
        here = []
        for f in range(F):
            planes = [
                pad[pl.ds(pl.multiple_of(f * span + (a0 + d) * C, C), C), :] for d in range(B + 2 * W)
            ]
            here.append(planes[W : W + B])
            axial.append(
                [
                    sum(c * (planes[W + p + k] - planes[W + p - k]) for k, c in enumerate(coeffs, start=1))
                    for p in range(B)
                ]
            )
        radial = jnp.dot(
            jnp.concatenate(here[3] + here[4], axis=0),
            band_ref[...],
            precision=HI,
            preferred_element_type=jnp.float32,
        )
        for p in range(B):
            rad3 = radial[p * C : (p + 1) * C]
            rad4 = radial[(B + p) * C : (B + p + 1) * C]
            div = axial[1][p] + circ(here[2][p]) + rad3
            rates = [
                mach * axial[0][p] + div,
                mach * axial[1][p] + axial[4][p],
                mach * axial[2][p] + circ(here[4][p]),
                mach * axial[3][p] + rad4,
                mach * axial[4][p] + div,
            ]
            sigma = damping * pml_ref[a0 + p].astype(jnp.float32)
            for f in range(F):
                rows = rows_of(f, a0 + p)
                value = -step_size * (rates[f] + sigma * here[f][p])
                if section:
                    value = value + section_a[section] * inc_ref[rows, :]
                out_ref[rows, :] = value
        return carry

    lax.fori_loop(0, A // B, step, 0)


def finish_kernel(
    section, last, offsets_ref, q_ref, part_ref, east_ref, odd_ref, rad_ref, own_ref, next_ref, *refs
):
    b = section_b[section]
    new_ref, inc_ref, *messages, low, high, faces = refs
    even = lax.rem(lax.axis_index("circ"), 2) == 0
    low_rad = lax.axis_index("rad") == 0
    rotor = lax.axis_index("half") == 0

    inside = slice(3 * A, 3 * A + 2 * W * A)
    low[inside, :] = jnp.where(even, odd_ref[...], east_ref[...])
    high[inside, :] = jnp.where(even, east_ref[...], odd_ref[...])
    sub = lax.broadcasted_iota(jnp.int32, (8, L), 0)

    def circ(a, g):
        lower = low[pl.ds((3 + g * W) * A + a, 8, stride=A), :]
        upper = high[pl.ds(g * W * A + a, 8, stride=A), :]
        return jnp.concatenate([jnp.where(sub < W, lower, 0.0), jnp.where(sub >= 8 - W, upper, 0.0)], axis=0)

    lane = lax.broadcasted_iota(jnp.int32, (GROUP, L), 1)
    rim_lanes = (lane >= jnp.where(low_rad, L - W, 0)) & (lane < jnp.where(low_rad, L, W))
    base = jnp.where(low_rad, L - W, 0)
    groups = A * C // GROUP

    def step(n, carry):
        rims = [
            jnp.where(rim_lanes, pltpu.roll(rad_ref[...], lax.rem(base + L - 8 * (n + g * groups), L), 1), 0.0)
            for g in range(2)
        ]
        for p in range(GROUP // C):
            a = n * (GROUP // C) + p
            div = circ(a, 0) + rims[0][p * C : (p + 1) * C]
            extra = [div, None, circ(a, 1), rims[1][p * C : (p + 1) * C], div]
            for f in range(F):
                rows = rows_of(f, a)
                value = part_ref[rows, :]
                if extra[f] is not None:
                    value = value - step_size * extra[f]
                inc_ref[rows, :] = value
                new_ref[rows, :] = q_ref[rows, :] + b * value
        return carry

    lax.fori_loop(0, groups, step, 0)

    for n in range(F * W):
        own, beyond = own_ref[n * C : (n + 1) * C, :], next_ref[n * C : (n + 1) * C, :]
        faces[2 * n * C : (2 * n + 1) * C, :] = jnp.where(rotor, own, beyond)
        faces[(2 * n + 1) * C : (2 * n + 2) * C, :] = jnp.where(rotor, beyond, own)
    shift = lax.rem(offsets_ref[section], C)
    start = jnp.where(rotor, shift, C - shift)
    sign = jnp.where(rotor, 1.0, -1.0)
    ghost = [[faces[pl.ds(2 * (f * W + m) * C + start, C), :] for m in range(W)] for f in range(F)]
    for i in range(W):
        a = jnp.where(rotor, A - 1 - i, i)
        axial = [sign * total_of([coeffs[k - 1] * ghost[f][k - 1 - i] for k in range(i + 1, W + 1)]) for f in range(F)]
        extra = [
            mach * axial[0] + axial[1],
            mach * axial[1] + axial[4],
            mach * axial[2],
            mach * axial[3],
            mach * axial[4] + axial[1],
        ]
        for f in range(F):
            rows = rows_of(f, a)
            delta = -step_size * extra[f]
            inc_ref[rows, :] += delta
            new_ref[rows, :] += b * delta
    if not last:
        pack(new_ref, *messages)


def swap_faces(face, blocks):
    count = lax.axis_size("circ")
    pairs = []
    for i in range(count):
        j = (i + blocks) % count
        pairs += [(2 * i, 2 * j + 1), (2 * j + 1, 2 * i)]
    return lax.ppermute(face, ("circ", "half"), pairs)


def exchange(messages, blocks):
    east, odd, rad, face = messages
    count = lax.axis_size("circ")
    return (
        lax.ppermute(east, "circ", [(i, i ^ 1) for i in range(count)]),
        lax.ppermute(odd, "circ", [(i, (i + (1 if i % 2 else -1)) % count) for i in range(count)]),
        lax.ppermute(rad, "rad", [(0, 1), (1, 0)]),
        swap_faces(face, blocks),
        swap_faces(face, blocks + 1),
    )


def local_terms(section, q, inc, pml_zone):
    return pl.pallas_call(
        functools.partial(local_kernel, section),
        out_shape=FIELDS,
        in_specs=[SM] + [VM] * (3 if section else 2),
        out_specs=VM,
        scratch_shapes=[pltpu.VMEM((F * (A + 2 * W) * C, L), jnp.float32)],
        compiler_params=PARAMS,
        cost_estimate=pl.CostEstimate(flops=20_000_000, bytes_accessed=3 * ROWS * L * 4, transcendentals=0),
        name=f"local{section}",
    )(pml_zone, band_matrix(), q, *([inc] if section else []))


def section_branch(section, blocks, q, inc, pml_zone, messages):
    arrived = exchange(messages, blocks)
    return local_terms(section, q, inc, pml_zone), arrived


def finish(section, offsets, q, part, arrived):
    last = section == SECTIONS - 1
    return pl.pallas_call(
        functools.partial(finish_kernel, section, last),
        out_shape=[FIELDS, FIELDS] + ([] if last else MESSAGES),
        in_specs=[SM] + [VM] * 7,
        out_specs=[VM] * (2 if last else 6),
        scratch_shapes=[
            pltpu.VMEM((16 * A, L), jnp.float32),
            pltpu.VMEM((16 * A, L), jnp.float32),
            pltpu.VMEM((2 * F * W * C, L), jnp.float32),
        ],
        compiler_params=PARAMS,
        name=f"finish{section}",
    )(offsets, q, part, *arrived)


def pack_kernel(q_ref, *messages):
    pack(q_ref, *messages)


def body(state, offsets, pml_zone):
    q = state.reshape(ROWS, L)
    inc = ()
    messages = pl.pallas_call(
        pack_kernel,
        out_shape=MESSAGES,
        in_specs=[VM],
        out_specs=[VM] * 4,
        compiler_params=PARAMS,
        name="pack",
    )(q)
    place = offsets // C
    kind = jnp.where(place == 0, 1, jnp.where(place == C, 2, 0))
    for section in range(SECTIONS):
        part, arrived = lax.switch(
            kind[section],
            [functools.partial(section_branch, section, blocks) for blocks in (-1, 0, C)],
            q,
            inc,
            pml_zone,
            messages,
        )
        q, inc, *messages = finish(section, offsets, q, part, arrived)
    return q.reshape(state.shape), inc.reshape(state.shape)


def solution(mesh):
    return jax.shard_map(
        body,
        mesh=mesh,
        in_specs=(P(None, "half", "circ", "rad"), P(), P("half")),
        out_specs=(P(None, "half", "circ", "rad"), P(None, "half", "circ", "rad")),
        check_vma=False,
    )
```

```python
import functools

import jax
import jax.numpy as jnp
import numpy as np
from jax import lax
from jax.experimental import pallas as pl
from jax.experimental.pallas import tpu as pltpu
from jax.sharding import PartitionSpec as P

SECTIONS = 3
F, A, C, L = 5, 48, 16, 128
ROWS = F * A * C
FIELD = A * C
W = 5
GROUP = 6 * C
PARAMS = pltpu.CompilerParams(vmem_limit_bytes=24 << 20)

coeffs = (0.872756993962, -0.286511173973, 0.09032000128, -0.020779405824, 0.002484594688)
mach = 0.3
step_size = 0.25
damping = 0.8
section_a = (0.0, -5.0 / 9.0, -153.0 / 128.0)
section_b = (1.0 / 3.0, 15.0 / 16.0, 8.0 / 15.0)
HI = lax.Precision.HIGHEST


def band_matrix():
    band = np.zeros((L, L), np.float32)
    for k, c in enumerate(coeffs, start=1):
        band += c * (np.eye(L, k=-k) - np.eye(L, k=k)).astype(np.float32)
    return band


def rows_of(f, a):
    return pl.ds(pl.multiple_of(f * FIELD + a * C, C), C)


def total_of(terms):
    total = terms[0]
    for term in terms[1:]:
        total = total + term
    return total


def pack(q_ref, east_ref, odd_ref, rad_ref, face_ref):
    even = lax.rem(lax.axis_index("circ"), 2) == 0
    low_rad = lax.axis_index("rad") == 0
    rotor = lax.axis_index("half") == 0
    for g, f in enumerate((2, 4)):
        head = [q_ref[pl.ds(f * FIELD + c, A, stride=C), :] for c in range(W)]
        tail = [q_ref[pl.ds(f * FIELD + C - W + c, A, stride=C), :] for c in range(W)]
        for i in range(W):
            onward = total_of([-coeffs[i + W - c - 1] * tail[c] for c in range(i, W)])
            back = total_of([coeffs[c + W - i - 1] * head[c] for c in range(i + 1)])
            row = (g * W + i) * A
            east_ref[row : row + A, :] = jnp.where(even, onward, back)
            odd_ref[row : row + A, :] = jnp.where(even, back, onward)

    lane = lax.broadcasted_iota(jnp.int32, (GROUP, L), 1)
    first = jnp.where(low_rad, W, 0)
    rims = jnp.zeros((GROUP, L), jnp.float32)
    for n in range(2 * FIELD // GROUP):
        x = q_ref[3 * FIELD + n * GROUP : 3 * FIELD + (n + 1) * GROUP, :]
        rims = jnp.where((lane >= 8 * n) & (lane < 8 * n + W), pltpu.roll(x, first + 8 * n, 1), rims)
    slot = lax.rem(lane, 8)
    onward, back = [], []
    for d in range(W):
        c = coeffs[W - 1 - d]
        onward.append(jnp.where(slot + d < W, -c, 0.0) * (pltpu.roll(rims, L - d, 1) if d else rims))
        back.append(jnp.where((slot >= d) & (slot < W), c, 0.0) * (pltpu.roll(rims, d, 1) if d else rims))
    rad_ref[...] = jnp.where(low_rad, total_of(onward), total_of(back))

    for f in range(F):
        for m in range(W):
            a = jnp.where(rotor, A - 1 - m, m)
            row = (f * W + m) * C
            face_ref[row : row + C, :] = q_ref[rows_of(f, a), :]


MESSAGES = [
    jax.ShapeDtypeStruct((2 * W * A, L), jnp.float32),
    jax.ShapeDtypeStruct((2 * W * A, L), jnp.float32),
    jax.ShapeDtypeStruct((GROUP, L), jnp.float32),
    jax.ShapeDtypeStruct((F * W * C, L), jnp.float32),
]
FIELDS = jax.ShapeDtypeStruct((ROWS, L), jnp.float32)
VM = pl.BlockSpec(memory_space=pltpu.VMEM)
SM = pl.BlockSpec(memory_space=pltpu.SMEM)


def local_kernel(section, pml_ref, band_ref, q_ref, *refs):
    inc_ref = refs[0] if section else None
    out_ref, pad = refs[-2:]
    zero = jnp.zeros((W * C, L), jnp.float32)
    span = (A + 2 * W) * C
    for f in range(F):
        pad[f * span : f * span + W * C, :] = zero
        pad[f * span + W * C : f * span + W * C + FIELD, :] = q_ref[f * FIELD : (f + 1) * FIELD, :]
        pad[(f + 1) * span - W * C : (f + 1) * span, :] = zero
    cell = lax.broadcasted_iota(jnp.int32, (C, L), 0)
    up = [jnp.where(cell < C - k, c, 0.0) for k, c in enumerate(coeffs, start=1)]
    down = [jnp.where(cell >= k, c, 0.0) for k, c in enumerate(coeffs, start=1)]

    def circ(x):
        total = None
        for k in range(1, W + 1):
            term = up[k - 1] * pltpu.roll(x, C - k, 0) - down[k - 1] * pltpu.roll(x, k, 0)
            total = term if total is None else total + term
        return total

    B = 4

    def step(n, carry):
        a0 = n * B
        axial = []
        here = []
        for f in range(F):
            planes = [
                pad[pl.ds(pl.multiple_of(f * span + (a0 + d) * C, C), C), :] for d in range(B + 2 * W)
            ]
            here.append(planes[W : W + B])
            axial.append(
                [
                    sum(c * (planes[W + p + k] - planes[W + p - k]) for k, c in enumerate(coeffs, start=1))
                    for p in range(B)
                ]
            )
        radial = jnp.dot(
            jnp.concatenate(here[3] + here[4], axis=0),
            band_ref[...],
            precision=HI,
            preferred_element_type=jnp.float32,
        )
        for p in range(B):
            rad3 = radial[p * C : (p + 1) * C]
            rad4 = radial[(B + p) * C : (B + p + 1) * C]
            div = axial[1][p] + circ(here[2][p]) + rad3
            rates = [
                mach * axial[0][p] + div,
                mach * axial[1][p] + axial[4][p],
                mach * axial[2][p] + circ(here[4][p]),
                mach * axial[3][p] + rad4,
                mach * axial[4][p] + div,
            ]
            sigma = damping * pml_ref[a0 + p].astype(jnp.float32)
            for f in range(F):
                rows = rows_of(f, a0 + p)
                value = -step_size * (rates[f] + sigma * here[f][p])
                if section:
                    value = value + section_a[section] * inc_ref[rows, :]
                out_ref[rows, :] = value
        return carry

    lax.fori_loop(0, A // B, step, 0)


def finish_kernel(
    section, last, offsets_ref, q_ref, part_ref, east_ref, odd_ref, rad_ref, own_ref, next_ref, *refs
):
    b = section_b[section]
    new_ref, inc_ref, *messages, low, high, faces = refs
    even = lax.rem(lax.axis_index("circ"), 2) == 0
    low_rad = lax.axis_index("rad") == 0
    rotor = lax.axis_index("half") == 0

    inside = slice(3 * A, 3 * A + 2 * W * A)
    low[inside, :] = jnp.where(even, odd_ref[...], east_ref[...])
    high[inside, :] = jnp.where(even, east_ref[...], odd_ref[...])
    sub = lax.broadcasted_iota(jnp.int32, (8, L), 0)

    def circ(a, g):
        lower = low[pl.ds((3 + g * W) * A + a, 8, stride=A), :]
        upper = high[pl.ds(g * W * A + a, 8, stride=A), :]
        return jnp.concatenate([jnp.where(sub < W, lower, 0.0), jnp.where(sub >= 8 - W, upper, 0.0)], axis=0)

    lane = lax.broadcasted_iota(jnp.int32, (GROUP, L), 1)
    rim_lanes = (lane >= jnp.where(low_rad, L - W, 0)) & (lane < jnp.where(low_rad, L, W))
    base = jnp.where(low_rad, L - W, 0)
    groups = A * C // GROUP

    def step(n, carry):
        rims = [
            jnp.where(rim_lanes, pltpu.roll(rad_ref[...], lax.rem(base + L - 8 * (n + g * groups), L), 1), 0.0)
            for g in range(2)
        ]
        for p in range(GROUP // C):
            a = n * (GROUP // C) + p
            div = circ(a, 0) + rims[0][p * C : (p + 1) * C]
            extra = [div, None, circ(a, 1), rims[1][p * C : (p + 1) * C], div]
            for f in range(F):
                rows = rows_of(f, a)
                value = part_ref[rows, :]
                if extra[f] is not None:
                    value = value - step_size * extra[f]
                inc_ref[rows, :] = value
                new_ref[rows, :] = q_ref[rows, :] + b * value
        return carry

    lax.fori_loop(0, groups, step, 0)

    for n in range(F * W):
        own, beyond = own_ref[n * C : (n + 1) * C, :], next_ref[n * C : (n + 1) * C, :]
        faces[2 * n * C : (2 * n + 1) * C, :] = jnp.where(rotor, own, beyond)
        faces[(2 * n + 1) * C : (2 * n + 2) * C, :] = jnp.where(rotor, beyond, own)
    shift = lax.rem(offsets_ref[section], C)
    start = jnp.where(rotor, shift, C - shift)
    sign = jnp.where(rotor, 1.0, -1.0)
    ghost = [[faces[pl.ds(2 * (f * W + m) * C + start, C), :] for m in range(W)] for f in range(F)]
    for i in range(W):
        a = jnp.where(rotor, A - 1 - i, i)
        axial = [sign * total_of([coeffs[k - 1] * ghost[f][k - 1 - i] for k in range(i + 1, W + 1)]) for f in range(F)]
        extra = [
            mach * axial[0] + axial[1],
            mach * axial[1] + axial[4],
            mach * axial[2],
            mach * axial[3],
            mach * axial[4] + axial[1],
        ]
        for f in range(F):
            rows = rows_of(f, a)
            delta = -step_size * extra[f]
            inc_ref[rows, :] += delta
            new_ref[rows, :] += b * delta
    if not last:
        pack(new_ref, *messages)


def swap_faces(face, blocks):
    count = lax.axis_size("circ")
    pairs = []
    for i in range(count):
        j = (i + blocks) % count
        pairs += [(2 * i, 2 * j + 1), (2 * j + 1, 2 * i)]
    return lax.ppermute(face, ("circ", "half"), pairs)


def exchange_rims(messages):
    east, odd, rad, _ = messages
    count = lax.axis_size("circ")
    return (
        lax.ppermute(east, "circ", [(i, i ^ 1) for i in range(count)]),
        lax.ppermute(odd, "circ", [(i, (i + (1 if i % 2 else -1)) % count) for i in range(count)]),
        lax.ppermute(rad, "rad", [(0, 1), (1, 0)]),
    )


def local_terms(section, q, inc, pml_zone):
    return pl.pallas_call(
        functools.partial(local_kernel, section),
        out_shape=FIELDS,
        in_specs=[SM] + [VM] * (3 if section else 2),
        out_specs=VM,
        scratch_shapes=[pltpu.VMEM((F * (A + 2 * W) * C, L), jnp.float32)],
        compiler_params=PARAMS,
        cost_estimate=pl.CostEstimate(flops=20_000_000, bytes_accessed=3 * ROWS * L * 4, transcendentals=0),
        name=f"local{section}",
    )(pml_zone, band_matrix(), q, *([inc] if section else []))


def section_branch(section, blocks, q, inc, pml_zone, face):
    return local_terms(section, q, inc, pml_zone), swap_faces(face, blocks), swap_faces(face, blocks + 1)


def finish(section, offsets, q, part, arrived):
    last = section == SECTIONS - 1
    return pl.pallas_call(
        functools.partial(finish_kernel, section, last),
        out_shape=[FIELDS, FIELDS] + ([] if last else MESSAGES),
        in_specs=[SM] + [VM] * 7,
        out_specs=[VM] * (2 if last else 6),
        scratch_shapes=[
            pltpu.VMEM((16 * A, L), jnp.float32),
            pltpu.VMEM((16 * A, L), jnp.float32),
            pltpu.VMEM((2 * F * W * C, L), jnp.float32),
        ],
        compiler_params=PARAMS,
        name=f"finish{section}",
    )(offsets, q, part, *arrived)


def enter_kernel(offsets_ref, state_ref, *refs):
    *messages, kind0, kind1, kind2, q_ref, sems = refs
    copies = []
    for n, f in enumerate((2, 4, 3)):
        rows = pl.ds(f * FIELD, FIELD)
        copies.append(pltpu.make_async_copy(state_ref.at[rows], q_ref.at[rows], sems.at[n]))
    edge = jnp.where(lax.axis_index("half") == 0, (A - W) * C, 0)
    for f in (0, 1):
        rows = pl.ds(pl.multiple_of(f * FIELD + edge, C), W * C)
        copies.append(pltpu.make_async_copy(state_ref.at[rows], q_ref.at[rows], sems.at[3 + f]))
    for copy in copies:
        copy.start()
    for section, kind in enumerate((kind0, kind1, kind2)):
        place = lax.div(offsets_ref[section], C)
        kind[0] = jnp.where(place == 0, 1, jnp.where(place == C, 2, 0))
    for copy in copies:
        copy.wait()
    pack(q_ref, *messages)


def first_branch(blocks, q, offsets, pml_zone, messages):
    rims = exchange_rims(messages)
    part, own, beyond = section_branch(0, blocks, q, (), pml_zone, messages[3])
    return finish(0, offsets, q, part, (*rims, own, beyond))


def body(state, offsets, pml_zone):
    q = state.reshape(ROWS, L)
    flag = jax.ShapeDtypeStruct((1,), jnp.int32)
    rest = pl.pallas_call(
        enter_kernel,
        out_shape=MESSAGES + [flag] * SECTIONS,
        in_specs=[SM, pl.BlockSpec(memory_space=pltpu.HBM)],
        out_specs=[VM] * 4 + [SM] * SECTIONS,
        scratch_shapes=[pltpu.VMEM((ROWS, L), jnp.float32), pltpu.SemaphoreType.DMA((W,))],
        compiler_params=PARAMS,
        name="enter",
    )(offsets, pltpu.with_memory_space_constraint(q, pltpu.HBM))
    messages, kinds = rest[:4], rest[4:]
    shifts = (-1, 0, C)
    q, inc, *messages = lax.switch(
        kinds[0][0], [functools.partial(first_branch, blocks) for blocks in shifts], q, offsets, pml_zone, messages
    )
    for section in range(1, SECTIONS):
        rims = exchange_rims(messages)
        part, own, beyond = lax.switch(
            kinds[section][0],
            [functools.partial(section_branch, section, blocks) for blocks in shifts],
            q,
            inc,
            pml_zone,
            messages[3],
        )
        q, inc, *messages = finish(section, offsets, q, part, (*rims, own, beyond))
    return q.reshape(state.shape), inc.reshape(state.shape)


def solution(mesh):
    return jax.shard_map(
        body,
        mesh=mesh,
        in_specs=(P(None, "half", "circ", "rad"), P(), P("half")),
        out_specs=(P(None, "half", "circ", "rad"), P(None, "half", "circ", "rad")),
        check_vma=False,
    )
```

```python
import functools

import jax
import jax.numpy as jnp
import numpy as np
from jax import lax
from jax.experimental import pallas as pl
from jax.experimental.pallas import tpu as pltpu
from jax.sharding import PartitionSpec as P

SECTIONS = 3
F, A, C, L = 5, 48, 16, 128
ROWS = F * A * C
FIELD = A * C
W = 5
GROUP = 6 * C
PARAMS = pltpu.CompilerParams(vmem_limit_bytes=24 << 20)

coeffs = (0.872756993962, -0.286511173973, 0.09032000128, -0.020779405824, 0.002484594688)
mach = 0.3
step_size = 0.25
damping = 0.8
section_a = (0.0, -5.0 / 9.0, -153.0 / 128.0)
section_b = (1.0 / 3.0, 15.0 / 16.0, 8.0 / 15.0)
HI = lax.Precision.HIGHEST


def band_matrix():
    band = np.zeros((L, L), np.float32)
    for k, c in enumerate(coeffs, start=1):
        band += c * (np.eye(L, k=-k) - np.eye(L, k=k)).astype(np.float32)
    return band


def rows_of(f, a):
    return pl.ds(pl.multiple_of(f * FIELD + a * C, C), C)


def total_of(terms):
    total = terms[0]
    for term in terms[1:]:
        total = total + term
    return total


def cells_of(ref, f, first):
    return [ref[pl.ds(f * FIELD + first + c, A, stride=C), :] for c in range(W)]


def contributions(cells, upward):
    added = []
    for i in range(W):
        onward = total_of([-coeffs[i + W - c - 1] * cells[c] for c in range(i, W)])
        back = total_of([coeffs[c + W - i - 1] * cells[c] for c in range(i + 1)])
        added.append(jnp.where(upward, onward, back))
    return added


def is_even():
    return lax.rem(lax.axis_index("circ"), 2) == 0


def sides():
    even = is_even()
    return (jnp.where(even, C - W, 0), even), (jnp.where(even, 0, C - W), jnp.logical_not(even))


def pack_rims(q_ref, east_ref, odd_ref):
    for out_ref, (first, upward) in zip((east_ref, odd_ref), sides()):
        for g, f in enumerate((2, 4)):
            for i, added in enumerate(contributions(cells_of(q_ref, f, first), upward)):
                out_ref[(g * W + i) * A : (g * W + i + 1) * A, :] = added


def pack_rad(q_ref, rad_ref):
    low_rad = lax.axis_index("rad") == 0
    lane = lax.broadcasted_iota(jnp.int32, (GROUP, L), 1)
    first = jnp.where(low_rad, W, 0)
    rims = jnp.zeros((GROUP, L), jnp.float32)
    for n in range(2 * FIELD // GROUP):
        x = q_ref[3 * FIELD + n * GROUP : 3 * FIELD + (n + 1) * GROUP, :]
        rims = jnp.where((lane >= 8 * n) & (lane < 8 * n + W), pltpu.roll(x, first + 8 * n, 1), rims)
    slot = lax.rem(lane, 8)
    onward, back = [], []
    for d in range(W):
        c = coeffs[W - 1 - d]
        onward.append(jnp.where(slot + d < W, -c, 0.0) * (pltpu.roll(rims, L - d, 1) if d else rims))
        back.append(jnp.where((slot >= d) & (slot < W), c, 0.0) * (pltpu.roll(rims, d, 1) if d else rims))
    rad_ref[...] = jnp.where(low_rad, total_of(onward), total_of(back))


def interface_planes():
    rotor = lax.axis_index("half") == 0
    return [jnp.where(rotor, A - 1 - m, m) for m in range(W)]


def pack_faces(q_ref, face_ref):
    for f in range(F):
        for m, a in enumerate(interface_planes()):
            row = (f * W + m) * C
            face_ref[row : row + C, :] = q_ref[rows_of(f, a), :]


RIM = jax.ShapeDtypeStruct((2 * W * A, L), jnp.float32)
RIMS = jax.ShapeDtypeStruct((4 * W * A, L), jnp.float32)
RAD = jax.ShapeDtypeStruct((GROUP, L), jnp.float32)
FACE = jax.ShapeDtypeStruct((F * W * C, L), jnp.float32)
FIELDS = jax.ShapeDtypeStruct((ROWS, L), jnp.float32)
VM = pl.BlockSpec(memory_space=pltpu.VMEM)
SM = pl.BlockSpec(memory_space=pltpu.SMEM)
ANY = pl.BlockSpec(memory_space=pl.ANY)


def local_kernel(section, pml_ref, band_ref, q_ref, *refs):
    inc_ref = refs[0] if section else None
    *outs, pad = refs[1:] if section else refs
    out_ref = outs[0]
    zero = jnp.zeros((W * C, L), jnp.float32)
    span = (A + 2 * W) * C
    for f in range(F):
        pad[f * span : f * span + W * C, :] = zero
        pad[f * span + W * C : f * span + W * C + FIELD, :] = q_ref[f * FIELD : (f + 1) * FIELD, :]
        pad[(f + 1) * span - W * C : (f + 1) * span, :] = zero
    cell = lax.broadcasted_iota(jnp.int32, (C, L), 0)
    up = [jnp.where(cell < C - k, c, 0.0) for k, c in enumerate(coeffs, start=1)]
    down = [jnp.where(cell >= k, c, 0.0) for k, c in enumerate(coeffs, start=1)]

    def circ(x):
        total = None
        for k in range(1, W + 1):
            term = up[k - 1] * pltpu.roll(x, C - k, 0) - down[k - 1] * pltpu.roll(x, k, 0)
            total = term if total is None else total + term
        return total

    B = 4

    def step(n, carry):
        a0 = n * B
        axial = []
        here = []
        for f in range(F):
            planes = [
                pad[pl.ds(pl.multiple_of(f * span + (a0 + d) * C, C), C), :] for d in range(B + 2 * W)
            ]
            here.append(planes[W : W + B])
            axial.append(
                [
                    sum(c * (planes[W + p + k] - planes[W + p - k]) for k, c in enumerate(coeffs, start=1))
                    for p in range(B)
                ]
            )
        radial = jnp.dot(
            jnp.concatenate(here[3] + here[4], axis=0),
            band_ref[...],
            precision=HI,
            preferred_element_type=jnp.float32,
        )
        for p in range(B):
            rad3 = radial[p * C : (p + 1) * C]
            rad4 = radial[(B + p) * C : (B + p + 1) * C]
            div = axial[1][p] + circ(here[2][p]) + rad3
            rates = [
                mach * axial[0][p] + div,
                mach * axial[1][p] + axial[4][p],
                mach * axial[2][p] + circ(here[4][p]),
                mach * axial[3][p] + rad4,
                mach * axial[4][p] + div,
            ]
            sigma = damping * pml_ref[a0 + p].astype(jnp.float32)
            for f in range(F):
                rows = rows_of(f, a0 + p)
                value = -step_size * (rates[f] + sigma * here[f][p])
                if section:
                    value = value + section_a[section] * inc_ref[rows, :]
                out_ref[rows, :] = value
        return carry

    lax.fori_loop(0, A // B, step, 0)
    if len(outs) > 1:
        for side, (first, _) in enumerate(sides()):
            for g, f in enumerate((2, 4)):
                for c, (now, part) in enumerate(zip(cells_of(q_ref, f, first), cells_of(out_ref, f, first))):
                    row = ((2 * side + g) * W + c) * A
                    outs[1][row : row + A, :] = now + section_b[section] * part
        for f in range(F):
            for m, a in enumerate(interface_planes()):
                row = (f * W + m) * C
                rows = rows_of(f, a)
                outs[2][row : row + C, :] = q_ref[rows, :] + section_b[section] * out_ref[rows, :]


def rim_rows(rad_ref, g, n):
    low_rad = lax.axis_index("rad") == 0
    lane = lax.broadcasted_iota(jnp.int32, (GROUP, L), 1)
    inside = (lane >= jnp.where(low_rad, L - W, 0)) & (lane < jnp.where(low_rad, L, W))
    base = jnp.where(low_rad, L - W, 0)
    turn = lax.rem(base + L - 8 * (n + g * (FIELD // GROUP)), L)
    return jnp.where(inside, pltpu.roll(rad_ref[...], turn, 1), 0.0)


def interface_terms(section, offsets_ref, own_ref, next_ref, faces, fields):
    rotor = lax.axis_index("half") == 0
    for f in fields:
        for n in range(f * W, f * W + W):
            own, beyond = own_ref[n * C : (n + 1) * C, :], next_ref[n * C : (n + 1) * C, :]
            faces[2 * n * C : (2 * n + 1) * C, :] = jnp.where(rotor, own, beyond)
            faces[(2 * n + 1) * C : (2 * n + 2) * C, :] = jnp.where(rotor, beyond, own)
    shift = lax.rem(offsets_ref[section], C)
    start = jnp.where(rotor, shift, C - shift)
    sign = jnp.where(rotor, 1.0, -1.0)
    ghost = {f: [faces[pl.ds(2 * (f * W + m) * C + start, C), :] for m in range(W)] for f in fields}
    planes = []
    for i in range(W):
        axial = {
            f: sign * total_of([coeffs[k - 1] * ghost[f][k - 1 - i] for k in range(i + 1, W + 1)]) for f in fields
        }
        extra = {f: mach * axial[f] for f in fields}
        for f, other in ((0, 1), (1, 4), (4, 1)):
            if f in fields:
                extra[f] = extra[f] + axial[other]
        planes.append((jnp.where(rotor, A - 1 - i, i), extra))
    return planes


def circ_reader(low, high, east_ref, odd_ref):
    even = is_even()

    inside = slice(3 * A, 3 * A + 2 * W * A)
    low[inside, :] = jnp.where(even, odd_ref[...], east_ref[...])
    high[inside, :] = jnp.where(even, east_ref[...], odd_ref[...])
    sub = lax.broadcasted_iota(jnp.int32, (8, L), 0)

    def circ(a, g):
        lower = low[pl.ds((3 + g * W) * A + a, 8, stride=A), :]
        upper = high[pl.ds(g * W * A + a, 8, stride=A), :]
        return jnp.concatenate([jnp.where(sub < W, lower, 0.0), jnp.where(sub >= 8 - W, upper, 0.0)], axis=0)

    return circ


def lead_kernel(
    section, offsets_ref, rim_ref, face_ref, east_ref, odd_ref, rad_ref, own_ref, next_ref, *refs
):
    to_east, to_odd, to_face, extra2, extra4, faces, low, high, rim4 = refs
    rotor = lax.axis_index("half") == 0
    circ = circ_reader(low, high, east_ref, odd_ref)
    rim4[...] = rim_rows(rad_ref, 1, jnp.where(rotor, FIELD // GROUP - 1, 0))
    scale = step_size * section_b[section]
    extra2[...] = jnp.zeros_like(extra2)
    for n in range(FIELD // GROUP):
        extra4[n * GROUP : (n + 1) * GROUP, :] = rim_rows(rad_ref, 0, n)
    for m, (a, extra) in enumerate(interface_terms(section, offsets_ref, own_ref, next_ref, faces, range(F))):
        rows = rows_of(0, a)
        rim3 = extra4[rows, :]
        beside = rim4[pl.ds(pl.multiple_of(jnp.where(rotor, GROUP // C - 1 - m, m) * C, C), C), :]
        div = circ(a, 0) + rim3
        deltas = [div + extra[0], extra[1], circ(a, 1) + extra[2], beside + extra[3], div + extra[4]]
        for f in range(F):
            row = (f * W + m) * C
            to_face[row : row + C, :] = face_ref[row : row + C, :] - scale * deltas[f]
        extra2[rows, :] += extra[2]
        extra4[rows, :] = rim3 + extra[4]
    for side, (first, upward) in enumerate(sides()):
        from_ref, out_ref = ((east_ref, to_east), (odd_ref, to_odd))[side]
        for g, beside in enumerate((extra2, extra4)):
            cells = []
            for c, other in enumerate(cells_of(beside, 0, first)):
                row = ((2 * side + g) * W + c) * A
                arrived = from_ref[((1 - g) * W + c) * A : ((1 - g) * W + c + 1) * A, :]
                cells.append(rim_ref[row : row + A, :] - scale * (arrived + other))
            for i, added in enumerate(contributions(cells, upward)):
                out_ref[(g * W + i) * A : (g * W + i + 1) * A, :] = added


def finish_kernel(
    section, last, offsets_ref, q_ref, part_ref, east_ref, odd_ref, rad_ref, own_ref, next_ref, *refs
):
    b = section_b[section]
    new_ref, inc_ref, *messages, low, high, faces = refs
    circ = circ_reader(low, high, east_ref, odd_ref)

    def step(n, carry):
        rims = [rim_rows(rad_ref, g, n) for g in range(2)]
        for p in range(GROUP // C):
            a = n * (GROUP // C) + p
            div = circ(a, 0) + rims[0][p * C : (p + 1) * C]
            extra = [div, None, circ(a, 1), rims[1][p * C : (p + 1) * C], div]
            for f in range(F):
                rows = rows_of(f, a)
                value = part_ref[rows, :]
                if extra[f] is not None:
                    value = value - step_size * extra[f]
                inc_ref[rows, :] = value
                new_ref[rows, :] = q_ref[rows, :] + b * value
        return carry

    lax.fori_loop(0, FIELD // GROUP, step, 0)

    for a, extra in interface_terms(section, offsets_ref, own_ref, next_ref, faces, range(F)):
        for f in range(F):
            rows = rows_of(f, a)
            delta = -step_size * extra[f]
            inc_ref[rows, :] += delta
            new_ref[rows, :] += b * delta
    if not last:
        pack_rad(new_ref, messages[0])


def swap_faces(face, blocks):
    count = lax.axis_size("circ")
    pairs = []
    for i in range(count):
        j = (i + blocks) % count
        pairs += [(2 * i, 2 * j + 1), (2 * j + 1, 2 * i)]
    return lax.ppermute(face, ("circ", "half"), pairs)


def send_east(east):
    return lax.ppermute(east, "circ", [(i, i ^ 1) for i in range(lax.axis_size("circ"))])


def send_odd(odd):
    count = lax.axis_size("circ")
    return lax.ppermute(odd, "circ", [(i, (i + (1 if i % 2 else -1)) % count) for i in range(count)])


def local_terms(section, q, inc, pml_zone):
    known = [] if section == SECTIONS - 1 else [RIMS, FACE]
    return pl.pallas_call(
        functools.partial(local_kernel, section),
        out_shape=[FIELDS] + known,
        in_specs=[SM] + [VM] * (3 if section else 2),
        out_specs=[VM] * (1 + len(known)),
        scratch_shapes=[pltpu.VMEM((F * (A + 2 * W) * C, L), jnp.float32)],
        compiler_params=PARAMS,
        cost_estimate=pl.CostEstimate(flops=20_000_000, bytes_accessed=3 * ROWS * L * 4, transcendentals=0),
        name=f"local{section}",
    )(pml_zone, band_matrix(), q, *([inc] if section else []))


def first_branch(blocks, q, pml_zone, face):
    own, beyond = swap_faces(face, blocks), swap_faces(face, blocks + 1)
    return local_terms(0, q, (), pml_zone), own, beyond


def section_branch(section, blocks, offsets, q, part, arrived, pml_zone, face):
    own, beyond = swap_faces(face, blocks), swap_faces(face, blocks + 1)
    q, inc, rad = finish(section - 1, offsets, q, part, arrived)
    return q, local_terms(section, q, inc, pml_zone), send_rad(rad), own, beyond


def send_rad(rad):
    return lax.ppermute(rad, "rad", [(0, 1), (1, 0)])


def lead(section, offsets, known, arrived):
    window = pltpu.VMEM((16 * A, L), jnp.float32)
    field = pltpu.VMEM((FIELD, L), jnp.float32)
    return pl.pallas_call(
        functools.partial(lead_kernel, section),
        out_shape=[RIM, RIM, FACE],
        in_specs=[SM] + [VM] * 7,
        out_specs=[VM] * 3,
        scratch_shapes=[field, field, pltpu.VMEM((2 * F * W * C, L), jnp.float32), window, window]
        + [pltpu.VMEM((GROUP, L), jnp.float32)],
        compiler_params=PARAMS,
        name=f"lead{section}",
    )(offsets, *known, *arrived)


def finish(section, offsets, q, part, arrived):
    last = section == SECTIONS - 1
    window = pltpu.VMEM((16 * A, L), jnp.float32)
    return pl.pallas_call(
        functools.partial(finish_kernel, section, last),
        out_shape=[FIELDS, FIELDS] + ([] if last else [RAD]),
        in_specs=[SM] + [VM] * 7,
        out_specs=[VM] * (2 if last else 3),
        scratch_shapes=[window, window, pltpu.VMEM((2 * F * W * C, L), jnp.float32)],
        compiler_params=PARAMS,
        cost_estimate=pl.CostEstimate(flops=8_000_000, bytes_accessed=4 * ROWS * L * 4, transcendentals=0),
        name=f"finish{section}",
    )(offsets, q, part, *arrived)


def enter_lead_kernel(offsets_ref, state_ref, east_ref, odd_ref, kind0, kind1, kind2, q_ref, sems):
    copies = []
    for n, f in enumerate((2, 4)):
        rows = pl.ds(f * FIELD, FIELD)
        copies.append(pltpu.make_async_copy(state_ref.at[rows], q_ref.at[rows], sems.at[n]))
    for copy in copies:
        copy.start()
    for section, kind in enumerate((kind0, kind1, kind2)):
        place = lax.div(offsets_ref[section], C)
        kind[0] = jnp.where(place == 0, 1, jnp.where(place == C, 2, 0))
    for copy in copies:
        copy.wait()
    pack_rims(q_ref, east_ref, odd_ref)


def enter_kernel(state_ref, sent_ref, *refs):
    *messages, q_ref, sems = refs
    copies = []
    for n, f in enumerate((3, 4)):
        rows = pl.ds(f * FIELD, FIELD)
        copies.append(pltpu.make_async_copy(state_ref.at[rows], q_ref.at[rows], sems.at[n]))
    edge = jnp.where(lax.axis_index("half") == 0, (A - W) * C, 0)
    for f in (0, 1, 2):
        rows = pl.ds(pl.multiple_of(f * FIELD + edge, C), W * C)
        copies.append(pltpu.make_async_copy(state_ref.at[rows], q_ref.at[rows], sems.at[2 + f]))
    for copy in copies:
        copy.start()
    for copy in copies:
        copy.wait()
    pack_rad(q_ref, messages[0])
    pack_faces(q_ref, messages[1])


def body(state, offsets, pml_zone):
    q = state.reshape(ROWS, L)
    held = pltpu.with_memory_space_constraint(q, pltpu.HBM)
    flag = jax.ShapeDtypeStruct((1,), jnp.int32)
    east, odd, *kinds = pl.pallas_call(
        enter_lead_kernel,
        out_shape=[RIM, RIM] + [flag] * SECTIONS,
        in_specs=[SM, pl.BlockSpec(memory_space=pltpu.HBM)],
        out_specs=[VM, VM] + [SM] * SECTIONS,
        scratch_shapes=[pltpu.VMEM((ROWS, L), jnp.float32), pltpu.SemaphoreType.DMA((2,))],
        compiler_params=PARAMS,
        name="enter_lead",
    )(offsets, held)
    rad, face = pl.pallas_call(
        enter_kernel,
        out_shape=[RAD, FACE],
        in_specs=[pl.BlockSpec(memory_space=pltpu.HBM), ANY],
        out_specs=[VM] * 2,
        scratch_shapes=[pltpu.VMEM((ROWS, L), jnp.float32), pltpu.SemaphoreType.DMA((W,))],
        compiler_params=PARAMS,
        cost_estimate=pl.CostEstimate(flops=8_000_000, bytes_accessed=4 * ROWS * L * 4, transcendentals=0),
        name="enter",
    )(held, east)
    shifts = (-1, 0, C)
    for section in range(SECTIONS):
        from_east, from_odd = send_east(east), send_odd(odd)
        if section == 0:
            from_rad = send_rad(rad)
            (part, *known), own, beyond = lax.switch(
                kinds[0][0], [functools.partial(first_branch, blocks) for blocks in shifts], q, pml_zone, face
            )
        else:
            q, (part, *known), from_rad, own, beyond = lax.switch(
                kinds[section][0],
                [functools.partial(section_branch, section, blocks) for blocks in shifts],
                offsets,
                q,
                part,
                arrived,
                pml_zone,
                face,
            )
        arrived = (from_east, from_odd, from_rad, own, beyond)
        if known:
            east, odd, face = lead(section, offsets, known, arrived)
    q, inc = finish(SECTIONS - 1, offsets, q, part, arrived)
    return q.reshape(state.shape), inc.reshape(state.shape)


def solution(mesh):
    return jax.shard_map(
        body,
        mesh=mesh,
        in_specs=(P(None, "half", "circ", "rad"), P(), P("half")),
        out_specs=(P(None, "half", "circ", "rad"), P(None, "half", "circ", "rad")),
        check_vma=False,
    )
```

```python
import functools

import jax
import jax.numpy as jnp
import ml_dtypes
import numpy as np
from jax import lax
from jax.experimental import pallas as pl
from jax.experimental.pallas import tpu as pltpu
from jax.sharding import PartitionSpec as P

SECTIONS = 3
F, A, C, L = 5, 48, 16, 128
ROWS = F * A * C
FIELD = A * C
W = 5
GROUP = 6 * C
PARAMS = pltpu.CompilerParams(vmem_limit_bytes=24 << 20)

coeffs = (0.872756993962, -0.286511173973, 0.09032000128, -0.020779405824, 0.002484594688)
mach = 0.3
step_size = 0.25
damping = 0.8
section_a = (0.0, -5.0 / 9.0, -153.0 / 128.0)
section_b = (1.0 / 3.0, 15.0 / 16.0, 8.0 / 15.0)


def split_matrices():
    band = np.zeros((L, L), np.float64)
    for k, c in enumerate(coeffs, start=1):
        band += c * (np.eye(L, k=k) - np.eye(L, k=-k))
    cells = np.kron(np.eye(L // C), band[:C, :C])

    def halves(x):
        high = x.astype(ml_dtypes.bfloat16)
        return high, (x - high.astype(np.float64)).astype(ml_dtypes.bfloat16)

    (rad_high, rad_low), (circ_high, circ_low) = halves(band.T), halves(cells)
    none = np.zeros_like(rad_high)
    return np.block([[rad_high, rad_low], [rad_high, none]]), np.block([[circ_high, circ_high], [circ_low, none]])


def split(x):
    high = x.astype(jnp.bfloat16)
    return high, (x - high.astype(jnp.float32)).astype(jnp.bfloat16)


def rows_of(f, a):
    return pl.ds(pl.multiple_of(f * FIELD + a * C, C), C)


def total_of(terms):
    total = terms[0]
    for term in terms[1:]:
        total = total + term
    return total


def cells_of(ref, f, first):
    return [ref[pl.ds(f * FIELD + first + c, A, stride=C), :] for c in range(W)]


def contributions(cells, upward):
    added = []
    for i in range(W):
        onward = total_of([-coeffs[i + W - c - 1] * cells[c] for c in range(i, W)])
        back = total_of([coeffs[c + W - i - 1] * cells[c] for c in range(i + 1)])
        added.append(jnp.where(upward, onward, back))
    return added


def is_even():
    return lax.rem(lax.axis_index("circ"), 2) == 0


def sides():
    even = is_even()
    return (jnp.where(even, C - W, 0), even), (jnp.where(even, 0, C - W), jnp.logical_not(even))


def pack_rims(q_ref, east_ref, odd_ref):
    for out_ref, (first, upward) in zip((east_ref, odd_ref), sides()):
        for g, f in enumerate((2, 4)):
            for i, added in enumerate(contributions(cells_of(q_ref, f, first), upward)):
                out_ref[(g * W + i) * A : (g * W + i + 1) * A, :] = added


def pack_rad(q_ref, rad_ref):
    low_rad = lax.axis_index("rad") == 0
    lane = lax.broadcasted_iota(jnp.int32, (GROUP, L), 1)
    first = jnp.where(low_rad, W, 0)
    rims = jnp.zeros((GROUP, L), jnp.float32)
    for n in range(2 * FIELD // GROUP):
        x = q_ref[3 * FIELD + n * GROUP : 3 * FIELD + (n + 1) * GROUP, :]
        rims = jnp.where((lane >= 8 * n) & (lane < 8 * n + W), pltpu.roll(x, first + 8 * n, 1), rims)
    slot = lax.rem(lane, 8)
    onward, back = [], []
    for d in range(W):
        c = coeffs[W - 1 - d]
        onward.append(jnp.where(slot + d < W, -c, 0.0) * (pltpu.roll(rims, L - d, 1) if d else rims))
        back.append(jnp.where((slot >= d) & (slot < W), c, 0.0) * (pltpu.roll(rims, d, 1) if d else rims))
    rad_ref[...] = jnp.where(low_rad, total_of(onward), total_of(back))


def interface_planes():
    rotor = lax.axis_index("half") == 0
    return [jnp.where(rotor, A - 1 - m, m) for m in range(W)]


def pack_faces(q_ref, face_ref):
    for f in range(F):
        for m, a in enumerate(interface_planes()):
            row = (f * W + m) * C
            face_ref[row : row + C, :] = q_ref[rows_of(f, a), :]


RIM = jax.ShapeDtypeStruct((2 * W * A, L), jnp.float32)
RIMS = jax.ShapeDtypeStruct((4 * W * A, L), jnp.float32)
RAD = jax.ShapeDtypeStruct((GROUP, L), jnp.float32)
FACE = jax.ShapeDtypeStruct((F * W * C, L), jnp.float32)
FIELDS = jax.ShapeDtypeStruct((ROWS, L), jnp.float32)
VM = pl.BlockSpec(memory_space=pltpu.VMEM)
SM = pl.BlockSpec(memory_space=pltpu.SMEM)
ANY = pl.BlockSpec(memory_space=pl.ANY)


def local_kernel(section, pml_ref, rad_ref, circ_ref, q_ref, *refs):
    inc_ref = refs[0] if section else None
    *outs, pad = refs[1:] if section else refs
    out_ref = outs[0]
    zero = jnp.zeros((W * C, L), jnp.float32)
    span = (A + 2 * W) * C
    for f in range(F):
        pad[f * span : f * span + W * C, :] = zero
        pad[f * span + W * C : f * span + W * C + FIELD, :] = q_ref[f * FIELD : (f + 1) * FIELD, :]
        pad[(f + 1) * span - W * C : (f + 1) * span, :] = zero
    B = L // C

    def step(n, carry):
        a0 = n * B
        axial = []
        here = []
        for f in range(F):
            planes = [
                pad[pl.ds(pl.multiple_of(f * span + (a0 + d) * C, C), C), :] for d in range(B + 2 * W)
            ]
            here.append(planes[W : W + B])
            axial.append(
                [
                    sum(c * (planes[W + p + k] - planes[W + p - k]) for k, c in enumerate(coeffs, start=1))
                    for p in range(B)
                ]
            )
        halves = {f: split(jnp.concatenate(here[f], axis=0)) for f in (2, 3, 4)}
        lanes = [jnp.concatenate(halves[f], axis=1) for f in (3, 4)]
        radial = jnp.dot(jnp.concatenate(lanes, axis=0), rad_ref[...], preferred_element_type=jnp.float32)
        radial = radial[:, :L] + radial[:, L:]
        cells = [jnp.concatenate([halves[2][h], halves[4][h]], axis=1) for h in range(2)]
        circ = jnp.dot(circ_ref[...], jnp.concatenate(cells, axis=0), preferred_element_type=jnp.float32)
        circ = circ[:L] + circ[L:]
        for p in range(B):
            rad3 = radial[p * C : (p + 1) * C]
            rad4 = radial[(B + p) * C : (B + p + 1) * C]
            circ2 = circ[p * C : (p + 1) * C, :L]
            circ4 = circ[p * C : (p + 1) * C, L:]
            div = axial[1][p] + circ2 + rad3
            rates = [
                mach * axial[0][p] + div,
                mach * axial[1][p] + axial[4][p],
                mach * axial[2][p] + circ4,
                mach * axial[3][p] + rad4,
                mach * axial[4][p] + div,
            ]
            sigma = damping * pml_ref[a0 + p].astype(jnp.float32)
            for f in range(F):
                rows = rows_of(f, a0 + p)
                value = -step_size * (rates[f] + sigma * here[f][p])
                if section:
                    value = value + section_a[section] * inc_ref[rows, :]
                out_ref[rows, :] = value
        return carry

    lax.fori_loop(0, A // B, step, 0)
    if len(outs) > 1:
        for side, (first, _) in enumerate(sides()):
            for g, f in enumerate((2, 4)):
                for c, (now, part) in enumerate(zip(cells_of(q_ref, f, first), cells_of(out_ref, f, first))):
                    row = ((2 * side + g) * W + c) * A
                    outs[1][row : row + A, :] = now + section_b[section] * part
        for f in range(F):
            for m, a in enumerate(interface_planes()):
                row = (f * W + m) * C
                rows = rows_of(f, a)
                outs[2][row : row + C, :] = q_ref[rows, :] + section_b[section] * out_ref[rows, :]


def rim_rows(rad_ref, g, n):
    low_rad = lax.axis_index("rad") == 0
    lane = lax.broadcasted_iota(jnp.int32, (GROUP, L), 1)
    inside = (lane >= jnp.where(low_rad, L - W, 0)) & (lane < jnp.where(low_rad, L, W))
    base = jnp.where(low_rad, L - W, 0)
    turn = lax.rem(base + L - 8 * (n + g * (FIELD // GROUP)), L)
    return jnp.where(inside, pltpu.roll(rad_ref[...], turn, 1), 0.0)


def interface_terms(section, offsets_ref, own_ref, next_ref, faces, fields):
    rotor = lax.axis_index("half") == 0
    for f in fields:
        for n in range(f * W, f * W + W):
            own, beyond = own_ref[n * C : (n + 1) * C, :], next_ref[n * C : (n + 1) * C, :]
            faces[2 * n * C : (2 * n + 1) * C, :] = jnp.where(rotor, own, beyond)
            faces[(2 * n + 1) * C : (2 * n + 2) * C, :] = jnp.where(rotor, beyond, own)
    shift = lax.rem(offsets_ref[section], C)
    start = jnp.where(rotor, shift, C - shift)
    sign = jnp.where(rotor, 1.0, -1.0)
    ghost = {f: [faces[pl.ds(2 * (f * W + m) * C + start, C), :] for m in range(W)] for f in fields}
    planes = []
    for i in range(W):
        axial = {
            f: sign * total_of([coeffs[k - 1] * ghost[f][k - 1 - i] for k in range(i + 1, W + 1)]) for f in fields
        }
        extra = {f: mach * axial[f] for f in fields}
        for f, other in ((0, 1), (1, 4), (4, 1)):
            if f in fields:
                extra[f] = extra[f] + axial[other]
        planes.append((jnp.where(rotor, A - 1 - i, i), extra))
    return planes


def circ_reader(low, high, east_ref, odd_ref):
    even = is_even()

    inside = slice(3 * A, 3 * A + 2 * W * A)
    low[inside, :] = jnp.where(even, odd_ref[...], east_ref[...])
    high[inside, :] = jnp.where(even, east_ref[...], odd_ref[...])
    sub = lax.broadcasted_iota(jnp.int32, (8, L), 0)

    def circ(a, g):
        lower = low[pl.ds((3 + g * W) * A + a, 8, stride=A), :]
        upper = high[pl.ds(g * W * A + a, 8, stride=A), :]
        return jnp.concatenate([jnp.where(sub < W, lower, 0.0), jnp.where(sub >= 8 - W, upper, 0.0)], axis=0)

    return circ


def lead_kernel(
    section, offsets_ref, rim_ref, face_ref, east_ref, odd_ref, rad_ref, own_ref, next_ref, *refs
):
    to_east, to_odd, to_face, extra2, extra4, faces, low, high, rim4 = refs
    rotor = lax.axis_index("half") == 0
    circ = circ_reader(low, high, east_ref, odd_ref)
    rim4[...] = rim_rows(rad_ref, 1, jnp.where(rotor, FIELD // GROUP - 1, 0))
    scale = step_size * section_b[section]
    extra2[...] = jnp.zeros_like(extra2)
    for n in range(FIELD // GROUP):
        extra4[n * GROUP : (n + 1) * GROUP, :] = rim_rows(rad_ref, 0, n)
    for m, (a, extra) in enumerate(interface_terms(section, offsets_ref, own_ref, next_ref, faces, range(F))):
        rows = rows_of(0, a)
        rim3 = extra4[rows, :]
        beside = rim4[pl.ds(pl.multiple_of(jnp.where(rotor, GROUP // C - 1 - m, m) * C, C), C), :]
        div = circ(a, 0) + rim3
        deltas = [div + extra[0], extra[1], circ(a, 1) + extra[2], beside + extra[3], div + extra[4]]
        for f in range(F):
            row = (f * W + m) * C
            to_face[row : row + C, :] = face_ref[row : row + C, :] - scale * deltas[f]
        extra2[rows, :] += extra[2]
        extra4[rows, :] = rim3 + extra[4]
    for side, (first, upward) in enumerate(sides()):
        from_ref, out_ref = ((east_ref, to_east), (odd_ref, to_odd))[side]
        for g, beside in enumerate((extra2, extra4)):
            cells = []
            for c, other in enumerate(cells_of(beside, 0, first)):
                row = ((2 * side + g) * W + c) * A
                arrived = from_ref[((1 - g) * W + c) * A : ((1 - g) * W + c + 1) * A, :]
                cells.append(rim_ref[row : row + A, :] - scale * (arrived + other))
            for i, added in enumerate(contributions(cells, upward)):
                out_ref[(g * W + i) * A : (g * W + i + 1) * A, :] = added


def finish_kernel(
    section, last, offsets_ref, q_ref, part_ref, east_ref, odd_ref, rad_ref, own_ref, next_ref, *refs
):
    b = section_b[section]
    new_ref, inc_ref, *messages, low, high, faces = refs
    circ = circ_reader(low, high, east_ref, odd_ref)

    def step(n, carry):
        rims = [rim_rows(rad_ref, g, n) for g in range(2)]
        for p in range(GROUP // C):
            a = n * (GROUP // C) + p
            div = circ(a, 0) + rims[0][p * C : (p + 1) * C]
            extra = [div, None, circ(a, 1), rims[1][p * C : (p + 1) * C], div]
            for f in range(F):
                rows = rows_of(f, a)
                value = part_ref[rows, :]
                if extra[f] is not None:
                    value = value - step_size * extra[f]
                inc_ref[rows, :] = value
                new_ref[rows, :] = q_ref[rows, :] + b * value
        return carry

    lax.fori_loop(0, FIELD // GROUP, step, 0)

    for a, extra in interface_terms(section, offsets_ref, own_ref, next_ref, faces, range(F)):
        for f in range(F):
            rows = rows_of(f, a)
            delta = -step_size * extra[f]
            inc_ref[rows, :] += delta
            new_ref[rows, :] += b * delta
    if not last:
        pack_rad(new_ref, messages[0])


def swap_faces(face, blocks):
    count = lax.axis_size("circ")
    pairs = []
    for i in range(count):
        j = (i + blocks) % count
        pairs += [(2 * i, 2 * j + 1), (2 * j + 1, 2 * i)]
    return lax.ppermute(face, ("circ", "half"), pairs)


def send_east(east):
    return lax.ppermute(east, "circ", [(i, i ^ 1) for i in range(lax.axis_size("circ"))])


def send_odd(odd):
    count = lax.axis_size("circ")
    return lax.ppermute(odd, "circ", [(i, (i + (1 if i % 2 else -1)) % count) for i in range(count)])


def local_terms(section, q, inc, pml_zone):
    known = [] if section == SECTIONS - 1 else [RIMS, FACE]
    return pl.pallas_call(
        functools.partial(local_kernel, section),
        out_shape=[FIELDS] + known,
        in_specs=[SM] + [VM] * (4 if section else 3),
        out_specs=[VM] * (1 + len(known)),
        scratch_shapes=[pltpu.VMEM((F * (A + 2 * W) * C, L), jnp.float32)],
        compiler_params=PARAMS,
        cost_estimate=pl.CostEstimate(flops=20_000_000, bytes_accessed=3 * ROWS * L * 4, transcendentals=0),
        name=f"local{section}",
    )(pml_zone, *split_matrices(), q, *([inc] if section else []))


def first_branch(blocks, q, pml_zone, face):
    own, beyond = swap_faces(face, blocks), swap_faces(face, blocks + 1)
    return local_terms(0, q, (), pml_zone), own, beyond


def section_branch(section, blocks, offsets, q, part, arrived, pml_zone, face):
    own, beyond = swap_faces(face, blocks), swap_faces(face, blocks + 1)
    q, inc, rad = finish(section - 1, offsets, q, part, arrived)
    return q, local_terms(section, q, inc, pml_zone), send_rad(rad), own, beyond


def send_rad(rad):
    return lax.ppermute(rad, "rad", [(0, 1), (1, 0)])


def lead(section, offsets, known, arrived):
    window = pltpu.VMEM((16 * A, L), jnp.float32)
    field = pltpu.VMEM((FIELD, L), jnp.float32)
    return pl.pallas_call(
        functools.partial(lead_kernel, section),
        out_shape=[RIM, RIM, FACE],
        in_specs=[SM] + [VM] * 7,
        out_specs=[VM] * 3,
        scratch_shapes=[field, field, pltpu.VMEM((2 * F * W * C, L), jnp.float32), window, window]
        + [pltpu.VMEM((GROUP, L), jnp.float32)],
        compiler_params=PARAMS,
        name=f"lead{section}",
    )(offsets, *known, *arrived)


def finish(section, offsets, q, part, arrived):
    last = section == SECTIONS - 1
    window = pltpu.VMEM((16 * A, L), jnp.float32)
    return pl.pallas_call(
        functools.partial(finish_kernel, section, last),
        out_shape=[FIELDS, FIELDS] + ([] if last else [RAD]),
        in_specs=[SM] + [VM] * 7,
        out_specs=[VM] * (2 if last else 3),
        scratch_shapes=[window, window, pltpu.VMEM((2 * F * W * C, L), jnp.float32)],
        compiler_params=PARAMS,
        cost_estimate=pl.CostEstimate(flops=8_000_000, bytes_accessed=4 * ROWS * L * 4, transcendentals=0),
        name=f"finish{section}",
    )(offsets, q, part, *arrived)


def enter_lead_kernel(offsets_ref, state_ref, east_ref, odd_ref, kind0, kind1, kind2, q_ref, sems):
    copies = []
    for n, f in enumerate((2, 4)):
        rows = pl.ds(f * FIELD, FIELD)
        copies.append(pltpu.make_async_copy(state_ref.at[rows], q_ref.at[rows], sems.at[n]))
    for copy in copies:
        copy.start()
    for section, kind in enumerate((kind0, kind1, kind2)):
        place = lax.div(offsets_ref[section], C)
        kind[0] = jnp.where(place == 0, 1, jnp.where(place == C, 2, 0))
    for copy in copies:
        copy.wait()
    pack_rims(q_ref, east_ref, odd_ref)


def enter_kernel(state_ref, sent_ref, *refs):
    *messages, q_ref, sems = refs
    copies = []
    for n, f in enumerate((3, 4)):
        rows = pl.ds(f * FIELD, FIELD)
        copies.append(pltpu.make_async_copy(state_ref.at[rows], q_ref.at[rows], sems.at[n]))
    edge = jnp.where(lax.axis_index("half") == 0, (A - W) * C, 0)
    for f in (0, 1, 2):
        rows = pl.ds(pl.multiple_of(f * FIELD + edge, C), W * C)
        copies.append(pltpu.make_async_copy(state_ref.at[rows], q_ref.at[rows], sems.at[2 + f]))
    for copy in copies:
        copy.start()
    for copy in copies:
        copy.wait()
    pack_rad(q_ref, messages[0])
    pack_faces(q_ref, messages[1])


def body(state, offsets, pml_zone):
    q = state.reshape(ROWS, L)
    held = pltpu.with_memory_space_constraint(q, pltpu.HBM)
    flag = jax.ShapeDtypeStruct((1,), jnp.int32)
    east, odd, *kinds = pl.pallas_call(
        enter_lead_kernel,
        out_shape=[RIM, RIM] + [flag] * SECTIONS,
        in_specs=[SM, pl.BlockSpec(memory_space=pltpu.HBM)],
        out_specs=[VM, VM] + [SM] * SECTIONS,
        scratch_shapes=[pltpu.VMEM((ROWS, L), jnp.float32), pltpu.SemaphoreType.DMA((2,))],
        compiler_params=PARAMS,
        name="enter_lead",
    )(offsets, held)
    rad, face = pl.pallas_call(
        enter_kernel,
        out_shape=[RAD, FACE],
        in_specs=[pl.BlockSpec(memory_space=pltpu.HBM), ANY],
        out_specs=[VM] * 2,
        scratch_shapes=[pltpu.VMEM((ROWS, L), jnp.float32), pltpu.SemaphoreType.DMA((W,))],
        compiler_params=PARAMS,
        cost_estimate=pl.CostEstimate(flops=8_000_000, bytes_accessed=4 * ROWS * L * 4, transcendentals=0),
        name="enter",
    )(held, east)
    shifts = (-1, 0, C)
    for section in range(SECTIONS):
        from_east, from_odd = send_east(east), send_odd(odd)
        if section == 0:
            from_rad = send_rad(rad)
            (part, *known), own, beyond = lax.switch(
                kinds[0][0], [functools.partial(first_branch, blocks) for blocks in shifts], q, pml_zone, face
            )
        else:
            q, (part, *known), from_rad, own, beyond = lax.switch(
                kinds[section][0],
                [functools.partial(section_branch, section, blocks) for blocks in shifts],
                offsets,
                q,
                part,
                arrived,
                pml_zone,
                face,
            )
        arrived = (from_east, from_odd, from_rad, own, beyond)
        if known:
            east, odd, face = lead(section, offsets, known, arrived)
    q, inc = finish(SECTIONS - 1, offsets, q, part, arrived)
    return q.reshape(state.shape), inc.reshape(state.shape)


def solution(mesh):
    return jax.shard_map(
        body,
        mesh=mesh,
        in_specs=(P(None, "half", "circ", "rad"), P(), P("half")),
        out_specs=(P(None, "half", "circ", "rad"), P(None, "half", "circ", "rad")),
        check_vma=False,
    )
```

```python
import functools

import jax
import jax.numpy as jnp
import numpy as np
from jax import lax
from jax.experimental import pallas as pl
from jax.experimental.pallas import tpu as pltpu
from jax.sharding import PartitionSpec as P

SECTIONS = 3
F, A, C, L = 5, 48, 16, 128
ROWS = F * A * C
FIELD = A * C
W = 5
GROUP = 6 * C
PARAMS = pltpu.CompilerParams(vmem_limit_bytes=24 << 20)

coeffs = (0.872756993962, -0.286511173973, 0.09032000128, -0.020779405824, 0.002484594688)
mach = 0.3
step_size = 0.25
damping = 0.8
section_a = (0.0, -5.0 / 9.0, -153.0 / 128.0)
section_b = (1.0 / 3.0, 15.0 / 16.0, 8.0 / 15.0)
HI = lax.Precision.HIGHEST


def band_matrix():
    band = np.zeros((L, L), np.float32)
    for k, c in enumerate(coeffs, start=1):
        band += c * (np.eye(L, k=-k) - np.eye(L, k=k)).astype(np.float32)
    return band


def rows_of(f, a):
    return pl.ds(pl.multiple_of(f * FIELD + a * C, C), C)


def total_of(terms):
    total = terms[0]
    for term in terms[1:]:
        total = total + term
    return total


def cells_of(ref, f, first):
    return [ref[pl.ds(f * FIELD + first + c, A, stride=C), :] for c in range(W)]


def contributions(cells, upward):
    added = []
    for i in range(W):
        onward = total_of([-coeffs[i + W - c - 1] * cells[c] for c in range(i, W)])
        back = total_of([coeffs[c + W - i - 1] * cells[c] for c in range(i + 1)])
        added.append(jnp.where(upward, onward, back))
    return added


def is_even():
    return lax.rem(lax.axis_index("circ"), 2) == 0


def sides():
    even = is_even()
    return (jnp.where(even, C - W, 0), even), (jnp.where(even, 0, C - W), jnp.logical_not(even))


def pack_rims(q_ref, east_ref, odd_ref):
    for out_ref, (first, upward) in zip((east_ref, odd_ref), sides()):
        for g, f in enumerate((2, 4)):
            for i, added in enumerate(contributions(cells_of(q_ref, f, first), upward)):
                out_ref[(g * W + i) * A : (g * W + i + 1) * A, :] = added


def pack_rad(q_ref, rad_ref):
    low_rad = lax.axis_index("rad") == 0
    lane = lax.broadcasted_iota(jnp.int32, (GROUP, L), 1)
    first = jnp.where(low_rad, W, 0)
    rims = jnp.zeros((GROUP, L), jnp.float32)
    for n in range(2 * FIELD // GROUP):
        x = q_ref[3 * FIELD + n * GROUP : 3 * FIELD + (n + 1) * GROUP, :]
        rims = jnp.where((lane >= 8 * n) & (lane < 8 * n + W), pltpu.roll(x, first + 8 * n, 1), rims)
    slot = lax.rem(lane, 8)
    onward, back = [], []
    for d in range(W):
        c = coeffs[W - 1 - d]
        onward.append(jnp.where(slot + d < W, -c, 0.0) * (pltpu.roll(rims, L - d, 1) if d else rims))
        back.append(jnp.where((slot >= d) & (slot < W), c, 0.0) * (pltpu.roll(rims, d, 1) if d else rims))
    rad_ref[...] = jnp.where(low_rad, total_of(onward), total_of(back))


def interface_planes():
    rotor = lax.axis_index("half") == 0
    return [jnp.where(rotor, A - 1 - m, m) for m in range(W)]


def pack_faces(q_ref, face_ref):
    for f in range(F):
        for m, a in enumerate(interface_planes()):
            row = (f * W + m) * C
            face_ref[row : row + C, :] = q_ref[rows_of(f, a), :]


RIM = jax.ShapeDtypeStruct((2 * W * A, L), jnp.float32)
RIMS = jax.ShapeDtypeStruct((4 * W * A, L), jnp.float32)
RAD = jax.ShapeDtypeStruct((GROUP, L), jnp.float32)
FACE = jax.ShapeDtypeStruct((F * W * C, L), jnp.float32)
FIELDS = jax.ShapeDtypeStruct((ROWS, L), jnp.float32)
VM = pl.BlockSpec(memory_space=pltpu.VMEM)
SM = pl.BlockSpec(memory_space=pltpu.SMEM)
ANY = pl.BlockSpec(memory_space=pl.ANY)


def local_kernel(section, pml_ref, band_ref, q_ref, *refs):
    inc_ref = refs[0] if section else None
    *outs, pad = refs[1:] if section else refs
    out_ref = outs[0]
    zero = jnp.zeros((W * C, L), jnp.float32)
    span = (A + 2 * W) * C
    for f in range(F):
        pad[f * span : f * span + W * C, :] = zero
        pad[f * span + W * C : f * span + W * C + FIELD, :] = q_ref[f * FIELD : (f + 1) * FIELD, :]
        pad[(f + 1) * span - W * C : (f + 1) * span, :] = zero
    cell = lax.broadcasted_iota(jnp.int32, (C, L), 0)
    up = [jnp.where(cell < C - k, c, 0.0) for k, c in enumerate(coeffs, start=1)]
    down = [jnp.where(cell >= k, c, 0.0) for k, c in enumerate(coeffs, start=1)]

    def circ(x):
        total = None
        for k in range(1, W + 1):
            term = up[k - 1] * pltpu.roll(x, C - k, 0) - down[k - 1] * pltpu.roll(x, k, 0)
            total = term if total is None else total + term
        return total

    B = 8

    def step(n, carry):
        a0 = n * B
        axial = []
        here = []
        for f in range(F):
            planes = [
                pad[pl.ds(pl.multiple_of(f * span + (a0 + d) * C, C), C), :] for d in range(B + 2 * W)
            ]
            here.append(planes[W : W + B])
            axial.append(
                [
                    sum(c * (planes[W + p + k] - planes[W + p - k]) for k, c in enumerate(coeffs, start=1))
                    for p in range(B)
                ]
            )
        radial = jnp.dot(
            jnp.concatenate(here[3] + here[4], axis=0),
            band_ref[...],
            precision=HI,
            preferred_element_type=jnp.float32,
        )
        for p in range(B):
            rad3 = radial[p * C : (p + 1) * C]
            rad4 = radial[(B + p) * C : (B + p + 1) * C]
            div = axial[1][p] + circ(here[2][p]) + rad3
            rates = [
                mach * axial[0][p] + div,
                mach * axial[1][p] + axial[4][p],
                mach * axial[2][p] + circ(here[4][p]),
                mach * axial[3][p] + rad4,
                mach * axial[4][p] + div,
            ]
            sigma = damping * pml_ref[a0 + p].astype(jnp.float32)
            for f in range(F):
                rows = rows_of(f, a0 + p)
                value = -step_size * (rates[f] + sigma * here[f][p])
                if section:
                    value = value + section_a[section] * inc_ref[rows, :]
                out_ref[rows, :] = value
        return carry

    lax.fori_loop(0, A // B, step, 0)
    if len(outs) > 1:
        for side, (first, _) in enumerate(sides()):
            for g, f in enumerate((2, 4)):
                for c, (now, part) in enumerate(zip(cells_of(q_ref, f, first), cells_of(out_ref, f, first))):
                    row = ((2 * side + g) * W + c) * A
                    outs[1][row : row + A, :] = now + section_b[section] * part
        for f in range(F):
            for m, a in enumerate(interface_planes()):
                row = (f * W + m) * C
                rows = rows_of(f, a)
                outs[2][row : row + C, :] = q_ref[rows, :] + section_b[section] * out_ref[rows, :]


def rim_rows(rad_ref, g, n):
    low_rad = lax.axis_index("rad") == 0
    lane = lax.broadcasted_iota(jnp.int32, (GROUP, L), 1)
    inside = (lane >= jnp.where(low_rad, L - W, 0)) & (lane < jnp.where(low_rad, L, W))
    base = jnp.where(low_rad, L - W, 0)
    turn = lax.rem(base + L - 8 * (n + g * (FIELD // GROUP)), L)
    return jnp.where(inside, pltpu.roll(rad_ref[...], turn, 1), 0.0)


def interface_terms(section, offsets_ref, own_ref, next_ref, faces, fields):
    rotor = lax.axis_index("half") == 0
    for f in fields:
        for n in range(f * W, f * W + W):
            own, beyond = own_ref[n * C : (n + 1) * C, :], next_ref[n * C : (n + 1) * C, :]
            faces[2 * n * C : (2 * n + 1) * C, :] = jnp.where(rotor, own, beyond)
            faces[(2 * n + 1) * C : (2 * n + 2) * C, :] = jnp.where(rotor, beyond, own)
    shift = lax.rem(offsets_ref[section], C)
    start = jnp.where(rotor, shift, C - shift)
    sign = jnp.where(rotor, 1.0, -1.0)
    ghost = {f: [faces[pl.ds(2 * (f * W + m) * C + start, C), :] for m in range(W)] for f in fields}
    planes = []
    for i in range(W):
        axial = {
            f: sign * total_of([coeffs[k - 1] * ghost[f][k - 1 - i] for k in range(i + 1, W + 1)]) for f in fields
        }
        extra = {f: mach * axial[f] for f in fields}
        for f, other in ((0, 1), (1, 4), (4, 1)):
            if f in fields:
                extra[f] = extra[f] + axial[other]
        planes.append((jnp.where(rotor, A - 1 - i, i), extra))
    return planes


def circ_reader(low, high, east_ref, odd_ref):
    even = is_even()

    inside = slice(3 * A, 3 * A + 2 * W * A)
    low[inside, :] = jnp.where(even, odd_ref[...], east_ref[...])
    high[inside, :] = jnp.where(even, east_ref[...], odd_ref[...])
    sub = lax.broadcasted_iota(jnp.int32, (8, L), 0)

    def circ(a, g):
        lower = low[pl.ds((3 + g * W) * A + a, 8, stride=A), :]
        upper = high[pl.ds(g * W * A + a, 8, stride=A), :]
        return jnp.concatenate([jnp.where(sub < W, lower, 0.0), jnp.where(sub >= 8 - W, upper, 0.0)], axis=0)

    return circ


def lead_kernel(
    section, offsets_ref, rim_ref, face_ref, east_ref, odd_ref, rad_ref, own_ref, next_ref, *refs
):
    to_east, to_odd, to_face, extra2, extra4, faces, low, high, rim4 = refs
    rotor = lax.axis_index("half") == 0
    circ = circ_reader(low, high, east_ref, odd_ref)
    rim4[...] = rim_rows(rad_ref, 1, jnp.where(rotor, FIELD // GROUP - 1, 0))
    scale = step_size * section_b[section]
    extra2[...] = jnp.zeros_like(extra2)
    for n in range(FIELD // GROUP):
        extra4[n * GROUP : (n + 1) * GROUP, :] = rim_rows(rad_ref, 0, n)
    for m, (a, extra) in enumerate(interface_terms(section, offsets_ref, own_ref, next_ref, faces, range(F))):
        rows = rows_of(0, a)
        rim3 = extra4[rows, :]
        beside = rim4[pl.ds(pl.multiple_of(jnp.where(rotor, GROUP // C - 1 - m, m) * C, C), C), :]
        div = circ(a, 0) + rim3
        deltas = [div + extra[0], extra[1], circ(a, 1) + extra[2], beside + extra[3], div + extra[4]]
        for f in range(F):
            row = (f * W + m) * C
            to_face[row : row + C, :] = face_ref[row : row + C, :] - scale * deltas[f]
        extra2[rows, :] += extra[2]
        extra4[rows, :] = rim3 + extra[4]
    for side, (first, upward) in enumerate(sides()):
        from_ref, out_ref = ((east_ref, to_east), (odd_ref, to_odd))[side]
        for g, beside in enumerate((extra2, extra4)):
            cells = []
            for c, other in enumerate(cells_of(beside, 0, first)):
                row = ((2 * side + g) * W + c) * A
                arrived = from_ref[((1 - g) * W + c) * A : ((1 - g) * W + c + 1) * A, :]
                cells.append(rim_ref[row : row + A, :] - scale * (arrived + other))
            for i, added in enumerate(contributions(cells, upward)):
                out_ref[(g * W + i) * A : (g * W + i + 1) * A, :] = added


def finish_kernel(
    section, last, offsets_ref, q_ref, part_ref, east_ref, odd_ref, rad_ref, own_ref, next_ref, *refs
):
    b = section_b[section]
    new_ref, inc_ref, *messages, low, high, faces = refs
    circ = circ_reader(low, high, east_ref, odd_ref)

    def step(n, carry):
        rims = [rim_rows(rad_ref, g, n) for g in range(2)]
        for p in range(GROUP // C):
            a = n * (GROUP // C) + p
            div = circ(a, 0) + rims[0][p * C : (p + 1) * C]
            extra = [div, None, circ(a, 1), rims[1][p * C : (p + 1) * C], div]
            for f in range(F):
                rows = rows_of(f, a)
                value = part_ref[rows, :]
                if extra[f] is not None:
                    value = value - step_size * extra[f]
                inc_ref[rows, :] = value
                new_ref[rows, :] = q_ref[rows, :] + b * value
        return carry

    lax.fori_loop(0, FIELD // GROUP, step, 0)

    for a, extra in interface_terms(section, offsets_ref, own_ref, next_ref, faces, range(F)):
        for f in range(F):
            rows = rows_of(f, a)
            delta = -step_size * extra[f]
            inc_ref[rows, :] += delta
            new_ref[rows, :] += b * delta
    if not last:
        pack_rad(new_ref, messages[0])


def swap_faces(face, blocks):
    count = lax.axis_size("circ")
    pairs = []
    for i in range(count):
        j = (i + blocks) % count
        pairs += [(2 * i, 2 * j + 1), (2 * j + 1, 2 * i)]
    return lax.ppermute(face, ("circ", "half"), pairs)


def send_east(east):
    return lax.ppermute(east, "circ", [(i, i ^ 1) for i in range(lax.axis_size("circ"))])


def send_odd(odd):
    count = lax.axis_size("circ")
    return lax.ppermute(odd, "circ", [(i, (i + (1 if i % 2 else -1)) % count) for i in range(count)])


def local_terms(section, q, inc, pml_zone):
    known = [] if section == SECTIONS - 1 else [RIMS, FACE]
    return pl.pallas_call(
        functools.partial(local_kernel, section),
        out_shape=[FIELDS] + known,
        in_specs=[SM] + [VM] * (3 if section else 2),
        out_specs=[VM] * (1 + len(known)),
        scratch_shapes=[pltpu.VMEM((F * (A + 2 * W) * C, L), jnp.float32)],
        compiler_params=PARAMS,
        cost_estimate=pl.CostEstimate(flops=20_000_000, bytes_accessed=3 * ROWS * L * 4, transcendentals=0),
        name=f"local{section}",
    )(pml_zone, band_matrix(), q, *([inc] if section else []))


def first_branch(blocks, q, pml_zone, rad, face):
    own, beyond = swap_faces(face, blocks), swap_faces(face, blocks + 1)
    return local_terms(0, q, (), pml_zone), send_rad(rad), own, beyond


def section_branch(section, blocks, offsets, q, part, arrived, pml_zone, face):
    own, beyond = swap_faces(face, blocks), swap_faces(face, blocks + 1)
    q, inc, rad = finish(section - 1, offsets, q, part, arrived)
    return q, local_terms(section, q, inc, pml_zone), send_rad(rad), own, beyond


def send_rad(rad):
    return lax.ppermute(rad, "rad", [(0, 1), (1, 0)])


def lead(section, offsets, known, arrived):
    window = pltpu.VMEM((16 * A, L), jnp.float32)
    field = pltpu.VMEM((FIELD, L), jnp.float32)
    return pl.pallas_call(
        functools.partial(lead_kernel, section),
        out_shape=[RIM, RIM, FACE],
        in_specs=[SM] + [VM] * 7,
        out_specs=[VM] * 3,
        scratch_shapes=[field, field, pltpu.VMEM((2 * F * W * C, L), jnp.float32), window, window]
        + [pltpu.VMEM((GROUP, L), jnp.float32)],
        compiler_params=PARAMS,
        name=f"lead{section}",
    )(offsets, *known, *arrived)


def finish(section, offsets, q, part, arrived):
    last = section == SECTIONS - 1
    window = pltpu.VMEM((16 * A, L), jnp.float32)
    return pl.pallas_call(
        functools.partial(finish_kernel, section, last),
        out_shape=[FIELDS, FIELDS] + ([] if last else [RAD]),
        in_specs=[SM] + [VM] * 7,
        out_specs=[VM] * (2 if last else 3),
        scratch_shapes=[window, window, pltpu.VMEM((2 * F * W * C, L), jnp.float32)],
        compiler_params=PARAMS,
        cost_estimate=pl.CostEstimate(flops=8_000_000, bytes_accessed=4 * ROWS * L * 4, transcendentals=0),
        name=f"finish{section}",
    )(offsets, q, part, *arrived)


def enter_kernel(offsets_ref, state_ref, *refs):
    east_ref, odd_ref, rad_ref, face_ref, kind0, kind1, kind2, q_ref, sems = refs
    copies = []
    for n, f in enumerate((2, 4, 3)):
        rows = pl.ds(f * FIELD, FIELD)
        copies.append(pltpu.make_async_copy(state_ref.at[rows], q_ref.at[rows], sems.at[n]))
    edge = jnp.where(lax.axis_index("half") == 0, (A - W) * C, 0)
    for f in (0, 1):
        rows = pl.ds(pl.multiple_of(f * FIELD + edge, C), W * C)
        copies.append(pltpu.make_async_copy(state_ref.at[rows], q_ref.at[rows], sems.at[3 + f]))
    for copy in copies:
        copy.start()
    for section, kind in enumerate((kind0, kind1, kind2)):
        place = lax.div(offsets_ref[section], C)
        kind[0] = jnp.where(place == 0, 1, jnp.where(place == C, 2, 0))
    for copy in copies:
        copy.wait()
    pack_rims(q_ref, east_ref, odd_ref)
    pack_rad(q_ref, rad_ref)
    pack_faces(q_ref, face_ref)


def body(state, offsets, pml_zone):
    q = state.reshape(ROWS, L)
    flag = jax.ShapeDtypeStruct((1,), jnp.int32)
    east, odd, rad, face, *kinds = pl.pallas_call(
        enter_kernel,
        out_shape=[RIM, RIM, RAD, FACE] + [flag] * SECTIONS,
        in_specs=[SM, pl.BlockSpec(memory_space=pltpu.HBM)],
        out_specs=[VM] * 4 + [SM] * SECTIONS,
        scratch_shapes=[pltpu.VMEM((ROWS, L), jnp.float32), pltpu.SemaphoreType.DMA((W,))],
        compiler_params=PARAMS,
        name="enter",
    )(offsets, pltpu.with_memory_space_constraint(q, pltpu.HBM))
    shifts = (-1, 0, C)
    for section in range(SECTIONS):
        from_east, from_odd = send_east(east), send_odd(odd)
        if section == 0:
            (part, *known), from_rad, own, beyond = lax.switch(
                kinds[0][0], [functools.partial(first_branch, blocks) for blocks in shifts], q, pml_zone, rad, face
            )
        else:
            q, (part, *known), from_rad, own, beyond = lax.switch(
                kinds[section][0],
                [functools.partial(section_branch, section, blocks) for blocks in shifts],
                offsets,
                q,
                part,
                arrived,
                pml_zone,
                face,
            )
        arrived = (from_east, from_odd, from_rad, own, beyond)
        if known:
            east, odd, face = lead(section, offsets, known, arrived)
    q, inc = finish(SECTIONS - 1, offsets, q, part, arrived)
    return q.reshape(state.shape), inc.reshape(state.shape)


def solution(mesh):
    return jax.shard_map(
        body,
        mesh=mesh,
        in_specs=(P(None, "half", "circ", "rad"), P(), P("half")),
        out_specs=(P(None, "half", "circ", "rad"), P(None, "half", "circ", "rad")),
        check_vma=False,
    )
```

```python
import functools

import jax
import jax.numpy as jnp
import numpy as np
from jax import lax
from jax.experimental import pallas as pl
from jax.experimental.pallas import tpu as pltpu
from jax.sharding import PartitionSpec as P

SECTIONS = 3
F, A, C, L = 5, 48, 16, 128
ROWS = F * A * C
FIELD = A * C
W = 5
GROUP = 6 * C
PARAMS = pltpu.CompilerParams(vmem_limit_bytes=24 << 20)

coeffs = (0.872756993962, -0.286511173973, 0.09032000128, -0.020779405824, 0.002484594688)
mach = 0.3
step_size = 0.25
damping = 0.8
section_a = (0.0, -5.0 / 9.0, -153.0 / 128.0)
section_b = (1.0 / 3.0, 15.0 / 16.0, 8.0 / 15.0)
HI = lax.Precision.HIGHEST


def band_matrix():
    band = np.zeros((L, L), np.float32)
    for k, c in enumerate(coeffs, start=1):
        band += c * (np.eye(L, k=-k) - np.eye(L, k=k)).astype(np.float32)
    return band


def rows_of(f, a):
    return pl.ds(pl.multiple_of(f * FIELD + a * C, C), C)


def total_of(terms):
    total = terms[0]
    for term in terms[1:]:
        total = total + term
    return total


def cells_of(ref, f, first):
    return [ref[pl.ds(f * FIELD + first + c, A, stride=C), :] for c in range(W)]


def contributions(cells, upward):
    added = []
    for i in range(W):
        onward = total_of([-coeffs[i + W - c - 1] * cells[c] for c in range(i, W)])
        back = total_of([coeffs[c + W - i - 1] * cells[c] for c in range(i + 1)])
        added.append(jnp.where(upward, onward, back))
    return added


def is_even():
    return lax.rem(lax.axis_index("circ"), 2) == 0


def sides():
    even = is_even()
    return (jnp.where(even, C - W, 0), even), (jnp.where(even, 0, C - W), jnp.logical_not(even))


def pack_rims(q_ref, east_ref, odd_ref):
    for out_ref, (first, upward) in zip((east_ref, odd_ref), sides()):
        for g, f in enumerate((2, 4)):
            for i, added in enumerate(contributions(cells_of(q_ref, f, first), upward)):
                out_ref[(g * W + i) * A : (g * W + i + 1) * A, :] = added


def pack_rad(q_ref, rad_ref):
    low_rad = lax.axis_index("rad") == 0
    lane = lax.broadcasted_iota(jnp.int32, (GROUP, L), 1)
    first = jnp.where(low_rad, W, 0)
    rims = jnp.zeros((GROUP, L), jnp.float32)
    for n in range(2 * FIELD // GROUP):
        x = q_ref[3 * FIELD + n * GROUP : 3 * FIELD + (n + 1) * GROUP, :]
        rims = jnp.where((lane >= 8 * n) & (lane < 8 * n + W), pltpu.roll(x, first + 8 * n, 1), rims)
    slot = lax.rem(lane, 8)
    onward, back = [], []
    for d in range(W):
        c = coeffs[W - 1 - d]
        onward.append(jnp.where(slot + d < W, -c, 0.0) * (pltpu.roll(rims, L - d, 1) if d else rims))
        back.append(jnp.where((slot >= d) & (slot < W), c, 0.0) * (pltpu.roll(rims, d, 1) if d else rims))
    rad_ref[...] = jnp.where(low_rad, total_of(onward), total_of(back))


def interface_planes():
    rotor = lax.axis_index("half") == 0
    return [jnp.where(rotor, A - 1 - m, m) for m in range(W)]


def pack_faces(q_ref, face_ref):
    for f in range(F):
        for m, a in enumerate(interface_planes()):
            row = (f * W + m) * C
            face_ref[row : row + C, :] = q_ref[rows_of(f, a), :]


RIM = jax.ShapeDtypeStruct((2 * W * A, L), jnp.float32)
RIMS = jax.ShapeDtypeStruct((4 * W * A, L), jnp.float32)
RAD = jax.ShapeDtypeStruct((GROUP, L), jnp.float32)
FACE = jax.ShapeDtypeStruct((F * W * C, L), jnp.float32)
FIELDS = jax.ShapeDtypeStruct((ROWS, L), jnp.float32)
VM = pl.BlockSpec(memory_space=pltpu.VMEM)
SM = pl.BlockSpec(memory_space=pltpu.SMEM)
ANY = pl.BlockSpec(memory_space=pl.ANY)


def local_kernel(section, pml_ref, band_ref, q_ref, *refs):
    inc_ref = refs[0] if section else None
    *outs, pad = refs[1:] if section else refs
    out_ref = outs[0]
    zero = jnp.zeros((W * C, L), jnp.float32)
    span = (A + 2 * W) * C
    for f in range(F):
        pad[f * span : f * span + W * C, :] = zero
        pad[f * span + W * C : f * span + W * C + FIELD, :] = q_ref[f * FIELD : (f + 1) * FIELD, :]
        pad[(f + 1) * span - W * C : (f + 1) * span, :] = zero
    cell = lax.broadcasted_iota(jnp.int32, (C, L), 0)
    up = [jnp.where(cell < C - k, c, 0.0) for k, c in enumerate(coeffs, start=1)]
    down = [jnp.where(cell >= k, c, 0.0) for k, c in enumerate(coeffs, start=1)]

    def circ(x):
        total = None
        for k in range(1, W + 1):
            term = up[k - 1] * pltpu.roll(x, C - k, 0) - down[k - 1] * pltpu.roll(x, k, 0)
            total = term if total is None else total + term
        return total

    B = 12

    def step(n, carry):
        a0 = n * B
        axial = []
        here = []
        for f in range(F):
            planes = [
                pad[pl.ds(pl.multiple_of(f * span + (a0 + d) * C, C), C), :] for d in range(B + 2 * W)
            ]
            here.append(planes[W : W + B])
            axial.append(
                [
                    sum(c * (planes[W + p + k] - planes[W + p - k]) for k, c in enumerate(coeffs, start=1))
                    for p in range(B)
                ]
            )
        radial = jnp.dot(
            jnp.concatenate(here[3] + here[4], axis=0),
            band_ref[...],
            precision=HI,
            preferred_element_type=jnp.float32,
        )
        for p in range(B):
            rad3 = radial[p * C : (p + 1) * C]
            rad4 = radial[(B + p) * C : (B + p + 1) * C]
            div = axial[1][p] + circ(here[2][p]) + rad3
            rates = [
                mach * axial[0][p] + div,
                mach * axial[1][p] + axial[4][p],
                mach * axial[2][p] + circ(here[4][p]),
                mach * axial[3][p] + rad4,
                mach * axial[4][p] + div,
            ]
            sigma = damping * pml_ref[a0 + p].astype(jnp.float32)
            for f in range(F):
                rows = rows_of(f, a0 + p)
                value = -step_size * (rates[f] + sigma * here[f][p])
                if section:
                    value = value + section_a[section] * inc_ref[rows, :]
                out_ref[rows, :] = value
        return carry

    lax.fori_loop(0, A // B, step, 0)
    if len(outs) > 1:
        for side, (first, _) in enumerate(sides()):
            for g, f in enumerate((2, 4)):
                for c, (now, part) in enumerate(zip(cells_of(q_ref, f, first), cells_of(out_ref, f, first))):
                    row = ((2 * side + g) * W + c) * A
                    outs[1][row : row + A, :] = now + section_b[section] * part
        for f in range(F):
            for m, a in enumerate(interface_planes()):
                row = (f * W + m) * C
                rows = rows_of(f, a)
                outs[2][row : row + C, :] = q_ref[rows, :] + section_b[section] * out_ref[rows, :]


def rim_rows(rad_ref, g, n):
    low_rad = lax.axis_index("rad") == 0
    lane = lax.broadcasted_iota(jnp.int32, (GROUP, L), 1)
    inside = (lane >= jnp.where(low_rad, L - W, 0)) & (lane < jnp.where(low_rad, L, W))
    base = jnp.where(low_rad, L - W, 0)
    turn = lax.rem(base + L - 8 * (n + g * (FIELD // GROUP)), L)
    return jnp.where(inside, pltpu.roll(rad_ref[...], turn, 1), 0.0)


def interface_terms(section, offsets_ref, own_ref, next_ref, faces, fields):
    rotor = lax.axis_index("half") == 0
    for f in fields:
        for n in range(f * W, f * W + W):
            own, beyond = own_ref[n * C : (n + 1) * C, :], next_ref[n * C : (n + 1) * C, :]
            faces[2 * n * C : (2 * n + 1) * C, :] = jnp.where(rotor, own, beyond)
            faces[(2 * n + 1) * C : (2 * n + 2) * C, :] = jnp.where(rotor, beyond, own)
    shift = lax.rem(offsets_ref[section], C)
    start = jnp.where(rotor, shift, C - shift)
    sign = jnp.where(rotor, 1.0, -1.0)
    ghost = {f: [faces[pl.ds(2 * (f * W + m) * C + start, C), :] for m in range(W)] for f in fields}
    planes = []
    for i in range(W):
        axial = {
            f: sign * total_of([coeffs[k - 1] * ghost[f][k - 1 - i] for k in range(i + 1, W + 1)]) for f in fields
        }
        extra = {f: mach * axial[f] for f in fields}
        for f, other in ((0, 1), (1, 4), (4, 1)):
            if f in fields:
                extra[f] = extra[f] + axial[other]
        planes.append((jnp.where(rotor, A - 1 - i, i), extra))
    return planes


def circ_reader(low, high, east_ref, odd_ref):
    even = is_even()

    inside = slice(3 * A, 3 * A + 2 * W * A)
    low[inside, :] = jnp.where(even, odd_ref[...], east_ref[...])
    high[inside, :] = jnp.where(even, east_ref[...], odd_ref[...])
    sub = lax.broadcasted_iota(jnp.int32, (8, L), 0)

    def circ(a, g):
        lower = low[pl.ds((3 + g * W) * A + a, 8, stride=A), :]
        upper = high[pl.ds(g * W * A + a, 8, stride=A), :]
        return jnp.concatenate([jnp.where(sub < W, lower, 0.0), jnp.where(sub >= 8 - W, upper, 0.0)], axis=0)

    return circ


def lead_kernel(
    section, offsets_ref, rim_ref, face_ref, east_ref, odd_ref, rad_ref, own_ref, next_ref, *refs
):
    to_east, to_odd, to_face, extra2, extra4, faces, low, high, rim4 = refs
    rotor = lax.axis_index("half") == 0
    circ = circ_reader(low, high, east_ref, odd_ref)
    rim4[...] = rim_rows(rad_ref, 1, jnp.where(rotor, FIELD // GROUP - 1, 0))
    scale = step_size * section_b[section]
    extra2[...] = jnp.zeros_like(extra2)
    for n in range(FIELD // GROUP):
        extra4[n * GROUP : (n + 1) * GROUP, :] = rim_rows(rad_ref, 0, n)
    for m, (a, extra) in enumerate(interface_terms(section, offsets_ref, own_ref, next_ref, faces, range(F))):
        rows = rows_of(0, a)
        rim3 = extra4[rows, :]
        beside = rim4[pl.ds(pl.multiple_of(jnp.where(rotor, GROUP // C - 1 - m, m) * C, C), C), :]
        div = circ(a, 0) + rim3
        deltas = [div + extra[0], extra[1], circ(a, 1) + extra[2], beside + extra[3], div + extra[4]]
        for f in range(F):
            row = (f * W + m) * C
            to_face[row : row + C, :] = face_ref[row : row + C, :] - scale * deltas[f]
        extra2[rows, :] += extra[2]
        extra4[rows, :] = rim3 + extra[4]
    for side, (first, upward) in enumerate(sides()):
        from_ref, out_ref = ((east_ref, to_east), (odd_ref, to_odd))[side]
        for g, beside in enumerate((extra2, extra4)):
            cells = []
            for c, other in enumerate(cells_of(beside, 0, first)):
                row = ((2 * side + g) * W + c) * A
                arrived = from_ref[((1 - g) * W + c) * A : ((1 - g) * W + c + 1) * A, :]
                cells.append(rim_ref[row : row + A, :] - scale * (arrived + other))
            for i, added in enumerate(contributions(cells, upward)):
                out_ref[(g * W + i) * A : (g * W + i + 1) * A, :] = added


def finish_kernel(
    section, last, offsets_ref, q_ref, part_ref, east_ref, odd_ref, rad_ref, own_ref, next_ref, *refs
):
    b = section_b[section]
    new_ref, inc_ref, *messages, low, high, faces = refs
    circ = circ_reader(low, high, east_ref, odd_ref)

    def step(n, carry):
        rims = [rim_rows(rad_ref, g, n) for g in range(2)]
        for p in range(GROUP // C):
            a = n * (GROUP // C) + p
            div = circ(a, 0) + rims[0][p * C : (p + 1) * C]
            extra = [div, None, circ(a, 1), rims[1][p * C : (p + 1) * C], div]
            for f in range(F):
                rows = rows_of(f, a)
                value = part_ref[rows, :]
                if extra[f] is not None:
                    value = value - step_size * extra[f]
                inc_ref[rows, :] = value
                new_ref[rows, :] = q_ref[rows, :] + b * value
        return carry

    lax.fori_loop(0, FIELD // GROUP, step, 0, unroll=2)

    for a, extra in interface_terms(section, offsets_ref, own_ref, next_ref, faces, range(F)):
        for f in range(F):
            rows = rows_of(f, a)
            delta = -step_size * extra[f]
            inc_ref[rows, :] += delta
            new_ref[rows, :] += b * delta
    if not last:
        pack_rad(new_ref, messages[0])


def swap_faces(face, blocks):
    count = lax.axis_size("circ")
    pairs = []
    for i in range(count):
        j = (i + blocks) % count
        pairs += [(2 * i, 2 * j + 1), (2 * j + 1, 2 * i)]
    return lax.ppermute(face, ("circ", "half"), pairs)


def send_east(east):
    return lax.ppermute(east, "circ", [(i, i ^ 1) for i in range(lax.axis_size("circ"))])


def send_odd(odd):
    count = lax.axis_size("circ")
    return lax.ppermute(odd, "circ", [(i, (i + (1 if i % 2 else -1)) % count) for i in range(count)])


def local_terms(section, q, inc, pml_zone):
    known = [] if section == SECTIONS - 1 else [RIMS, FACE]
    return pl.pallas_call(
        functools.partial(local_kernel, section),
        out_shape=[FIELDS] + known,
        in_specs=[SM] + [VM] * (3 if section else 2),
        out_specs=[VM] * (1 + len(known)),
        scratch_shapes=[pltpu.VMEM((F * (A + 2 * W) * C, L), jnp.float32)],
        compiler_params=PARAMS,
        cost_estimate=pl.CostEstimate(flops=20_000_000, bytes_accessed=3 * ROWS * L * 4, transcendentals=0),
        name=f"local{section}",
    )(pml_zone, band_matrix(), q, *([inc] if section else []))


def first_branch(blocks, q, pml_zone, rad, face):
    own, beyond = swap_faces(face, blocks), swap_faces(face, blocks + 1)
    return local_terms(0, q, (), pml_zone), send_rad(rad), own, beyond


def section_branch(section, blocks, offsets, q, part, arrived, pml_zone, face):
    own, beyond = swap_faces(face, blocks), swap_faces(face, blocks + 1)
    q, inc, rad = finish(section - 1, offsets, q, part, arrived)
    return q, local_terms(section, q, inc, pml_zone), send_rad(rad), own, beyond


def send_rad(rad):
    return lax.ppermute(rad, "rad", [(0, 1), (1, 0)])


def lead(section, offsets, known, arrived):
    window = pltpu.VMEM((16 * A, L), jnp.float32)
    field = pltpu.VMEM((FIELD, L), jnp.float32)
    return pl.pallas_call(
        functools.partial(lead_kernel, section),
        out_shape=[RIM, RIM, FACE],
        in_specs=[SM] + [VM] * 7,
        out_specs=[VM] * 3,
        scratch_shapes=[field, field, pltpu.VMEM((2 * F * W * C, L), jnp.float32), window, window]
        + [pltpu.VMEM((GROUP, L), jnp.float32)],
        compiler_params=PARAMS,
        name=f"lead{section}",
    )(offsets, *known, *arrived)


def finish(section, offsets, q, part, arrived):
    last = section == SECTIONS - 1
    window = pltpu.VMEM((16 * A, L), jnp.float32)
    return pl.pallas_call(
        functools.partial(finish_kernel, section, last),
        out_shape=[FIELDS, FIELDS] + ([] if last else [RAD]),
        in_specs=[SM] + [VM] * 7,
        out_specs=[VM] * (2 if last else 3),
        scratch_shapes=[window, window, pltpu.VMEM((2 * F * W * C, L), jnp.float32)],
        compiler_params=PARAMS,
        cost_estimate=pl.CostEstimate(flops=8_000_000, bytes_accessed=4 * ROWS * L * 4, transcendentals=0),
        name=f"finish{section}",
    )(offsets, q, part, *arrived)


def enter_kernel(offsets_ref, state_ref, *refs):
    east_ref, odd_ref, rad_ref, face_ref, kind0, kind1, kind2, q_ref, sems = refs
    copies = []
    for n, f in enumerate((2, 4, 3)):
        rows = pl.ds(f * FIELD, FIELD)
        copies.append(pltpu.make_async_copy(state_ref.at[rows], q_ref.at[rows], sems.at[n]))
    edge = jnp.where(lax.axis_index("half") == 0, (A - W) * C, 0)
    for f in (0, 1):
        rows = pl.ds(pl.multiple_of(f * FIELD + edge, C), W * C)
        copies.append(pltpu.make_async_copy(state_ref.at[rows], q_ref.at[rows], sems.at[3 + f]))
    for copy in copies:
        copy.start()
    for section, kind in enumerate((kind0, kind1, kind2)):
        place = lax.div(offsets_ref[section], C)
        kind[0] = jnp.where(place == 0, 1, jnp.where(place == C, 2, 0))
    for copy in copies:
        copy.wait()
    pack_rims(q_ref, east_ref, odd_ref)
    pack_rad(q_ref, rad_ref)
    pack_faces(q_ref, face_ref)


def body(state, offsets, pml_zone):
    q = state.reshape(ROWS, L)
    flag = jax.ShapeDtypeStruct((1,), jnp.int32)
    east, odd, rad, face, *kinds = pl.pallas_call(
        enter_kernel,
        out_shape=[RIM, RIM, RAD, FACE] + [flag] * SECTIONS,
        in_specs=[SM, pl.BlockSpec(memory_space=pltpu.HBM)],
        out_specs=[VM] * 4 + [SM] * SECTIONS,
        scratch_shapes=[pltpu.VMEM((ROWS, L), jnp.float32), pltpu.SemaphoreType.DMA((W,))],
        compiler_params=PARAMS,
        name="enter",
    )(offsets, pltpu.with_memory_space_constraint(q, pltpu.HBM))
    shifts = (-1, 0, C)
    for section in range(SECTIONS):
        from_east, from_odd = send_east(east), send_odd(odd)
        if section == 0:
            (part, *known), from_rad, own, beyond = lax.switch(
                kinds[0][0], [functools.partial(first_branch, blocks) for blocks in shifts], q, pml_zone, rad, face
            )
        else:
            q, (part, *known), from_rad, own, beyond = lax.switch(
                kinds[section][0],
                [functools.partial(section_branch, section, blocks) for blocks in shifts],
                offsets,
                q,
                part,
                arrived,
                pml_zone,
                face,
            )
        arrived = (from_east, from_odd, from_rad, own, beyond)
        if known:
            east, odd, face = lead(section, offsets, known, arrived)
    q, inc = finish(SECTIONS - 1, offsets, q, part, arrived)
    return q.reshape(state.shape), inc.reshape(state.shape)


def solution(mesh):
    return jax.shard_map(
        body,
        mesh=mesh,
        in_specs=(P(None, "half", "circ", "rad"), P(), P("half")),
        out_specs=(P(None, "half", "circ", "rad"), P(None, "half", "circ", "rad")),
        check_vma=False,
    )
```

```python
import functools

import jax
import jax.numpy as jnp
import numpy as np
from jax import lax
from jax.experimental import pallas as pl
from jax.experimental.pallas import tpu as pltpu
from jax.sharding import PartitionSpec as P

SECTIONS = 3
F, A, C, L = 5, 48, 16, 128
ROWS = F * A * C
FIELD = A * C
W = 5
GROUP = 6 * C
PARAMS = pltpu.CompilerParams(vmem_limit_bytes=24 << 20)

coeffs = (0.872756993962, -0.286511173973, 0.09032000128, -0.020779405824, 0.002484594688)
mach = 0.3
step_size = 0.25
damping = 0.8
section_a = (0.0, -5.0 / 9.0, -153.0 / 128.0)
section_b = (1.0 / 3.0, 15.0 / 16.0, 8.0 / 15.0)
HI = lax.Precision.HIGHEST


def band_matrix():
    band = np.zeros((L, L), np.float32)
    for k, c in enumerate(coeffs, start=1):
        band += c * (np.eye(L, k=-k) - np.eye(L, k=k)).astype(np.float32)
    return band


def rows_of(f, a):
    return pl.ds(pl.multiple_of(f * FIELD + a * C, C), C)


def total_of(terms):
    total = terms[0]
    for term in terms[1:]:
        total = total + term
    return total


def cells_of(ref, f, first):
    return [ref[pl.ds(f * FIELD + first + c, A, stride=C), :] for c in range(W)]


def contributions(cells, upward):
    added = []
    for i in range(W):
        onward = total_of([-coeffs[i + W - c - 1] * cells[c] for c in range(i, W)])
        back = total_of([coeffs[c + W - i - 1] * cells[c] for c in range(i + 1)])
        added.append(jnp.where(upward, onward, back))
    return added


def is_even():
    return lax.rem(lax.axis_index("circ"), 2) == 0


def sides():
    even = is_even()
    return (jnp.where(even, C - W, 0), even), (jnp.where(even, 0, C - W), jnp.logical_not(even))


def pack_rims(q_ref, east_ref, odd_ref):
    for out_ref, (first, upward) in zip((east_ref, odd_ref), sides()):
        for g, f in enumerate((2, 4)):
            for i, added in enumerate(contributions(cells_of(q_ref, f, first), upward)):
                out_ref[(g * W + i) * A : (g * W + i + 1) * A, :] = added


def pack_rad(q_ref, rad_ref):
    low_rad = lax.axis_index("rad") == 0
    lane = lax.broadcasted_iota(jnp.int32, (GROUP, L), 1)
    first = jnp.where(low_rad, W, 0)
    rims = jnp.zeros((GROUP, L), jnp.float32)
    for n in range(2 * FIELD // GROUP):
        x = q_ref[3 * FIELD + n * GROUP : 3 * FIELD + (n + 1) * GROUP, :]
        rims = jnp.where((lane >= 8 * n) & (lane < 8 * n + W), pltpu.roll(x, first + 8 * n, 1), rims)
    slot = lax.rem(lane, 8)
    onward, back = [], []
    for d in range(W):
        c = coeffs[W - 1 - d]
        onward.append(jnp.where(slot + d < W, -c, 0.0) * (pltpu.roll(rims, L - d, 1) if d else rims))
        back.append(jnp.where((slot >= d) & (slot < W), c, 0.0) * (pltpu.roll(rims, d, 1) if d else rims))
    rad_ref[...] = jnp.where(low_rad, total_of(onward), total_of(back))


def interface_planes():
    rotor = lax.axis_index("half") == 0
    return [jnp.where(rotor, A - 1 - m, m) for m in range(W)]


def pack_faces(q_ref, face_ref):
    for f in range(F):
        for m, a in enumerate(interface_planes()):
            row = (f * W + m) * C
            face_ref[row : row + C, :] = q_ref[rows_of(f, a), :]


RIM = jax.ShapeDtypeStruct((2 * W * A, L), jnp.float32)
RIMS = jax.ShapeDtypeStruct((4 * W * A, L), jnp.float32)
RAD = jax.ShapeDtypeStruct((GROUP, L), jnp.float32)
FACE = jax.ShapeDtypeStruct((F * W * C, L), jnp.float32)
FIELDS = jax.ShapeDtypeStruct((ROWS, L), jnp.float32)
VM = pl.BlockSpec(memory_space=pltpu.VMEM)
SM = pl.BlockSpec(memory_space=pltpu.SMEM)
ANY = pl.BlockSpec(memory_space=pl.ANY)


def local_kernel(section, pml_ref, band_ref, q_ref, *refs):
    inc_ref = refs[0] if section else None
    *outs, pad = refs[1:] if section else refs
    out_ref = outs[0]
    zero = jnp.zeros((W * C, L), jnp.float32)
    span = (A + 2 * W) * C
    for f in range(F):
        pad[f * span : f * span + W * C, :] = zero
        pad[f * span + W * C : f * span + W * C + FIELD, :] = q_ref[f * FIELD : (f + 1) * FIELD, :]
        pad[(f + 1) * span - W * C : (f + 1) * span, :] = zero
    cell = lax.broadcasted_iota(jnp.int32, (C, L), 0)
    up = [jnp.where(cell < C - k, c, 0.0) for k, c in enumerate(coeffs, start=1)]
    down = [jnp.where(cell >= k, c, 0.0) for k, c in enumerate(coeffs, start=1)]

    def circ(x):
        total = None
        for k in range(1, W + 1):
            term = up[k - 1] * pltpu.roll(x, C - k, 0) - down[k - 1] * pltpu.roll(x, k, 0)
            total = term if total is None else total + term
        return total

    B = 12

    def step(n, carry):
        a0 = n * B
        axial = []
        here = []
        for f in range(F):
            planes = [
                pad[pl.ds(pl.multiple_of(f * span + (a0 + d) * C, C), C), :] for d in range(B + 2 * W)
            ]
            here.append(planes[W : W + B])
            axial.append(
                [
                    sum(c * (planes[W + p + k] - planes[W + p - k]) for k, c in enumerate(coeffs, start=1))
                    for p in range(B)
                ]
            )
        radial = jnp.dot(
            jnp.concatenate(here[3] + here[4], axis=0),
            band_ref[...],
            precision=HI,
            preferred_element_type=jnp.float32,
        )
        for p in range(B):
            rad3 = radial[p * C : (p + 1) * C]
            rad4 = radial[(B + p) * C : (B + p + 1) * C]
            div = axial[1][p] + circ(here[2][p]) + rad3
            rates = [
                mach * axial[0][p] + div,
                mach * axial[1][p] + axial[4][p],
                mach * axial[2][p] + circ(here[4][p]),
                mach * axial[3][p] + rad4,
                mach * axial[4][p] + div,
            ]
            sigma = damping * pml_ref[a0 + p].astype(jnp.float32)
            for f in range(F):
                rows = rows_of(f, a0 + p)
                value = -step_size * (rates[f] + sigma * here[f][p])
                if section:
                    value = value + section_a[section] * inc_ref[rows, :]
                out_ref[rows, :] = value
        return carry

    lax.fori_loop(0, A // B, step, 0)
    if len(outs) > 1:
        for side, (first, _) in enumerate(sides()):
            for g, f in enumerate((2, 4)):
                for c, (now, part) in enumerate(zip(cells_of(q_ref, f, first), cells_of(out_ref, f, first))):
                    row = ((2 * side + g) * W + c) * A
                    outs[1][row : row + A, :] = now + section_b[section] * part
        for f in range(F):
            for m, a in enumerate(interface_planes()):
                row = (f * W + m) * C
                rows = rows_of(f, a)
                outs[2][row : row + C, :] = q_ref[rows, :] + section_b[section] * out_ref[rows, :]


def rim_rows(rad_ref, g, n):
    low_rad = lax.axis_index("rad") == 0
    lane = lax.broadcasted_iota(jnp.int32, (GROUP, L), 1)
    inside = (lane >= jnp.where(low_rad, L - W, 0)) & (lane < jnp.where(low_rad, L, W))
    base = jnp.where(low_rad, L - W, 0)
    turn = lax.rem(base + L - 8 * (n + g * (FIELD // GROUP)), L)
    return jnp.where(inside, pltpu.roll(rad_ref[...], turn, 1), 0.0)


def interface_terms(section, offsets_ref, own_ref, next_ref, faces, fields):
    rotor = lax.axis_index("half") == 0
    for f in fields:
        for n in range(f * W, f * W + W):
            own, beyond = own_ref[n * C : (n + 1) * C, :], next_ref[n * C : (n + 1) * C, :]
            faces[2 * n * C : (2 * n + 1) * C, :] = jnp.where(rotor, own, beyond)
            faces[(2 * n + 1) * C : (2 * n + 2) * C, :] = jnp.where(rotor, beyond, own)
    shift = lax.rem(offsets_ref[section], C)
    start = jnp.where(rotor, shift, C - shift)
    sign = jnp.where(rotor, 1.0, -1.0)
    ghost = {f: [faces[pl.ds(2 * (f * W + m) * C + start, C), :] for m in range(W)] for f in fields}
    planes = []
    for i in range(W):
        axial = {
            f: sign * total_of([coeffs[k - 1] * ghost[f][k - 1 - i] for k in range(i + 1, W + 1)]) for f in fields
        }
        extra = {f: mach * axial[f] for f in fields}
        for f, other in ((0, 1), (1, 4), (4, 1)):
            if f in fields:
                extra[f] = extra[f] + axial[other]
        planes.append((jnp.where(rotor, A - 1 - i, i), extra))
    return planes


def circ_reader(low, high, east_ref, odd_ref):
    even = is_even()

    inside = slice(3 * A, 3 * A + 2 * W * A)
    low[inside, :] = jnp.where(even, odd_ref[...], east_ref[...])
    high[inside, :] = jnp.where(even, east_ref[...], odd_ref[...])
    sub = lax.broadcasted_iota(jnp.int32, (8, L), 0)

    def circ(a, g):
        lower = low[pl.ds((3 + g * W) * A + a, 8, stride=A), :]
        upper = high[pl.ds(g * W * A + a, 8, stride=A), :]
        return jnp.concatenate([jnp.where(sub < W, lower, 0.0), jnp.where(sub >= 8 - W, upper, 0.0)], axis=0)

    return circ


def lead_kernel(
    section, offsets_ref, rim_ref, face_ref, east_ref, odd_ref, rad_ref, own_ref, next_ref, *refs
):
    to_east, to_odd, to_face, extra2, extra4, faces, low, high, rim4 = refs
    rotor = lax.axis_index("half") == 0
    circ = circ_reader(low, high, east_ref, odd_ref)
    rim4[...] = rim_rows(rad_ref, 1, jnp.where(rotor, FIELD // GROUP - 1, 0))
    scale = step_size * section_b[section]
    extra2[...] = jnp.zeros_like(extra2)
    for n in range(FIELD // GROUP):
        extra4[n * GROUP : (n + 1) * GROUP, :] = rim_rows(rad_ref, 0, n)
    for m, (a, extra) in enumerate(interface_terms(section, offsets_ref, own_ref, next_ref, faces, range(F))):
        rows = rows_of(0, a)
        rim3 = extra4[rows, :]
        beside = rim4[pl.ds(pl.multiple_of(jnp.where(rotor, GROUP // C - 1 - m, m) * C, C), C), :]
        div = circ(a, 0) + rim3
        deltas = [div + extra[0], extra[1], circ(a, 1) + extra[2], beside + extra[3], div + extra[4]]
        for f in range(F):
            row = (f * W + m) * C
            to_face[row : row + C, :] = face_ref[row : row + C, :] - scale * deltas[f]
        extra2[rows, :] += extra[2]
        extra4[rows, :] = rim3 + extra[4]
    for side, (first, upward) in enumerate(sides()):
        from_ref, out_ref = ((east_ref, to_east), (odd_ref, to_odd))[side]
        for g, beside in enumerate((extra2, extra4)):
            cells = []
            for c, other in enumerate(cells_of(beside, 0, first)):
                row = ((2 * side + g) * W + c) * A
                arrived = from_ref[((1 - g) * W + c) * A : ((1 - g) * W + c + 1) * A, :]
                cells.append(rim_ref[row : row + A, :] - scale * (arrived + other))
            for i, added in enumerate(contributions(cells, upward)):
                out_ref[(g * W + i) * A : (g * W + i + 1) * A, :] = added


def finish_kernel(
    section, last, offsets_ref, q_ref, part_ref, east_ref, odd_ref, rad_ref, own_ref, next_ref, *refs
):
    b = section_b[section]
    new_ref, inc_ref, *messages, low, high, faces = refs
    circ = circ_reader(low, high, east_ref, odd_ref)

    def step(n, carry):
        rims = [rim_rows(rad_ref, g, n) for g in range(2)]
        for p in range(GROUP // C):
            a = n * (GROUP // C) + p
            div = circ(a, 0) + rims[0][p * C : (p + 1) * C]
            extra = [div, None, circ(a, 1), rims[1][p * C : (p + 1) * C], div]
            for f in range(F):
                rows = rows_of(f, a)
                value = part_ref[rows, :]
                if extra[f] is not None:
                    value = value - step_size * extra[f]
                inc_ref[rows, :] = value
                new_ref[rows, :] = q_ref[rows, :] + b * value
        return carry

    lax.fori_loop(0, FIELD // GROUP, step, 0, unroll=2)

    for a, extra in interface_terms(section, offsets_ref, own_ref, next_ref, faces, range(F)):
        for f in range(F):
            rows = rows_of(f, a)
            delta = -step_size * extra[f]
            inc_ref[rows, :] += delta
            new_ref[rows, :] += b * delta
    if not last:
        pack_rad(new_ref, messages[0])


def swap_faces(face, blocks):
    count = lax.axis_size("circ")
    pairs = []
    for i in range(count):
        j = (i + blocks) % count
        pairs += [(2 * i, 2 * j + 1), (2 * j + 1, 2 * i)]
    return lax.ppermute(face, ("circ", "half"), pairs)


def send_east(east):
    return lax.ppermute(east, "circ", [(i, i ^ 1) for i in range(lax.axis_size("circ"))])


def send_odd(odd):
    count = lax.axis_size("circ")
    return lax.ppermute(odd, "circ", [(i, (i + (1 if i % 2 else -1)) % count) for i in range(count)])


def local_terms(section, q, inc, pml_zone):
    known = [] if section == SECTIONS - 1 else [RIMS, FACE]
    return pl.pallas_call(
        functools.partial(local_kernel, section),
        out_shape=[FIELDS] + known,
        in_specs=[SM] + [VM] * (3 if section else 2),
        out_specs=[VM] * (1 + len(known)),
        scratch_shapes=[pltpu.VMEM((F * (A + 2 * W) * C, L), jnp.float32)],
        compiler_params=PARAMS,
        cost_estimate=pl.CostEstimate(flops=20_000_000, bytes_accessed=3 * ROWS * L * 4, transcendentals=0),
        name=f"local{section}",
    )(pml_zone, band_matrix(), q, *([inc] if section else []))


def first_branch(blocks, q, pml_zone, rad, face):
    own, beyond = swap_faces(face, blocks), swap_faces(face, blocks + 1)
    return local_terms(0, q, (), pml_zone), send_rad(rad), own, beyond


def section_branch(section, blocks, offsets, q, part, arrived, pml_zone, face):
    own, beyond = swap_faces(face, blocks), swap_faces(face, blocks + 1)
    q, inc, rad = finish(section - 1, offsets, q, part, arrived)
    return q, local_terms(section, q, inc, pml_zone), send_rad(rad), own, beyond


def send_rad(rad):
    return lax.ppermute(rad, "rad", [(0, 1), (1, 0)])


def lead(section, offsets, known, arrived):
    window = pltpu.VMEM((16 * A, L), jnp.float32)
    field = pltpu.VMEM((FIELD, L), jnp.float32)
    return pl.pallas_call(
        functools.partial(lead_kernel, section),
        out_shape=[RIM, RIM, FACE],
        in_specs=[SM] + [VM] * 7,
        out_specs=[VM] * 3,
        scratch_shapes=[field, field, pltpu.VMEM((2 * F * W * C, L), jnp.float32), window, window]
        + [pltpu.VMEM((GROUP, L), jnp.float32)],
        compiler_params=PARAMS,
        name=f"lead{section}",
    )(offsets, *known, *arrived)


def finish(section, offsets, q, part, arrived):
    last = section == SECTIONS - 1
    window = pltpu.VMEM((16 * A, L), jnp.float32)
    return pl.pallas_call(
        functools.partial(finish_kernel, section, last),
        out_shape=[FIELDS, FIELDS] + ([] if last else [RAD]),
        in_specs=[SM] + [VM] * 7,
        out_specs=[VM] * (2 if last else 3),
        scratch_shapes=[window, window, pltpu.VMEM((2 * F * W * C, L), jnp.float32)],
        compiler_params=PARAMS,
        cost_estimate=pl.CostEstimate(flops=8_000_000, bytes_accessed=4 * ROWS * L * 4, transcendentals=0),
        name=f"finish{section}",
    )(offsets, q, part, *arrived)


def enter_kernel(offsets_ref, state_ref, *refs):
    east_ref, odd_ref, rad_ref, face_ref, kind0, kind1, kind2, q_ref, sems = refs
    copies = []
    for n, f in enumerate((2, 4, 3)):
        rows = pl.ds(f * FIELD, FIELD)
        copies.append(pltpu.make_async_copy(state_ref.at[rows], q_ref.at[rows], sems.at[n]))
    edge = jnp.where(lax.axis_index("half") == 0, (A - W) * C, 0)
    for f in (0, 1):
        rows = pl.ds(pl.multiple_of(f * FIELD + edge, C), W * C)
        copies.append(pltpu.make_async_copy(state_ref.at[rows], q_ref.at[rows], sems.at[3 + f]))
    for copy in copies:
        copy.start()
    for section, kind in enumerate((kind0, kind1, kind2)):
        place = lax.div(offsets_ref[section], C)
        kind[0] = jnp.where(place == 0, 1, jnp.where(place == C, 2, 0))
    copies[0].wait()
    copies[1].wait()
    pack_rims(q_ref, east_ref, odd_ref)
    copies[2].wait()
    pack_rad(q_ref, rad_ref)
    copies[3].wait()
    copies[4].wait()
    pack_faces(q_ref, face_ref)


def body(state, offsets, pml_zone):
    q = state.reshape(ROWS, L)
    flag = jax.ShapeDtypeStruct((1,), jnp.int32)
    east, odd, rad, face, *kinds = pl.pallas_call(
        enter_kernel,
        out_shape=[RIM, RIM, RAD, FACE] + [flag] * SECTIONS,
        in_specs=[SM, pl.BlockSpec(memory_space=pltpu.HBM)],
        out_specs=[VM] * 4 + [SM] * SECTIONS,
        scratch_shapes=[pltpu.VMEM((ROWS, L), jnp.float32), pltpu.SemaphoreType.DMA((W,))],
        compiler_params=PARAMS,
        name="enter",
    )(offsets, pltpu.with_memory_space_constraint(q, pltpu.HBM))
    shifts = (-1, 0, C)
    for section in range(SECTIONS):
        from_east, from_odd = send_east(east), send_odd(odd)
        if section == 0:
            (part, *known), from_rad, own, beyond = lax.switch(
                kinds[0][0], [functools.partial(first_branch, blocks) for blocks in shifts], q, pml_zone, rad, face
            )
        else:
            q, (part, *known), from_rad, own, beyond = lax.switch(
                kinds[section][0],
                [functools.partial(section_branch, section, blocks) for blocks in shifts],
                offsets,
                q,
                part,
                arrived,
                pml_zone,
                face,
            )
        arrived = (from_east, from_odd, from_rad, own, beyond)
        if known:
            east, odd, face = lead(section, offsets, known, arrived)
    q, inc = finish(SECTIONS - 1, offsets, q, part, arrived)
    return q.reshape(state.shape), inc.reshape(state.shape)


def solution(mesh):
    return jax.shard_map(
        body,
        mesh=mesh,
        in_specs=(P(None, "half", "circ", "rad"), P(), P("half")),
        out_specs=(P(None, "half", "circ", "rad"), P(None, "half", "circ", "rad")),
        check_vma=False,
    )
```
